32 devices in a mesh: dp: 4 (over x, core), tensor: 8 (over z, y).
Axes of the slice: x: 2, y: 2, z: 4, core: 2. Of those that a mesh axis runs over, the one named last changes fastest.
Arguments:
- stream: bfloat16 [1536, 2560], P(('dp', 'tensor')), may hold values from -26 to 26
- lengths: int32 [4, 6], P('dp'), may hold values from 16 to 192, as said below
- page_table: int32 [96], P('dp'), may hold values from 0 to 95, as said below
- request_prompt: int32 [64], P('dp'), may hold values from 0 to 23
- attn_gain: bfloat16 [2560], replicated, may hold values from 0.099609375 to 1.8984375
- query_gain: bfloat16 [128], replicated, may hold values from 0.5 to 10, as said below
- key_gain: bfloat16 [128], replicated, may hold values from 0.5 to 10, as said below
- mlp_gain: bfloat16 [2560], replicated, may hold values from 0.099609375 to 1.8984375
- w_query: bfloat16 [2560, 4096], P(None, 'tensor'), may hold values from -0.125 to 0.125
- key_value_weight: bfloat16 [2560, 2048], P(None, 'tensor'), may hold values from -0.125 to 0.125
- w_out: bfloat16 [4096, 2560], P('tensor'), may hold values from -0.5 to 0.5
- w_gate: bfloat16 [2560, 9728], P(None, 'tensor'), may hold values from -0.125 to 0.125
- w_up: bfloat16 [2560, 9728], P(None, 'tensor'), may hold values from -0.125 to 0.125
- w_down: bfloat16 [9728, 2560], P('tensor'), may hold values from -0.0625 to 0.0625
Outputs:
- layer_out: bfloat16 [1536, 2560], P(('dp', 'tensor'))
- paged_key_value_cache: bfloat16 [96, 16, 2048], P('dp', None, 'tensor')
- request_state: bfloat16 [64, 2560], P('dp', 'tensor')
The draws below stay inside these ranges and needn't reach their ends.
Inputs may be any that keep to these rules, and one draw needn't show every extreme that they name: Every length is a multiple of 16; each batch's lengths add up to 384, and the largest length of each batch is exactly 192. page_table is a permutation of all global slots; slot v belongs to owner v // 24, and each batch writes exactly 6 pages to each owner. `query_gain`: positive gains. `key_gain`: positive gains.
All inputs are finite; a program needn't handle non-finite values.
Results may differ from the reference program's by a relative error of at most 0.02.
The reference program's roundings to bfloat16 on the way count: a program that leaves them out, or rounds other values in their place, can miss the bound.
Values may be sent and summed in bfloat16 or wider, within the bound.
A program may use at most 128 MiB of HBM per device.

```python
import math
import jax
import jax.numpy as jnp
from jax import lax

MODEL_WIDTH = 2560
QUERY_HEADS = 32
KEY_VALUE_HEADS = 8
HEAD_SIZE = 128
FF = 9728
PAGE_TOKENS = 16
NPROMPT = 6
NREQ = 16
BATCH_TOKENS = 384
BATCH_COUNT = 4
ROWS = 1536
PAGES_PER_BATCH = 24
CAPP = 6
N_TENSOR = 8


def draw_stream(key, part):
    key = jax.random.fold_in(key, 5)
    base_key, row_key, col_key = jax.random.split(key, 3)
    row_scale = jnp.exp(jax.random.uniform(row_key, (ROWS, 1), minval=math.log(0.3), maxval=math.log(3.0)))
    col_scale = jnp.exp(jax.random.uniform(col_key, (1, MODEL_WIDTH), minval=math.log(0.5), maxval=math.log(2.0)))
    base = jnp.clip(jax.random.normal(base_key, (ROWS, MODEL_WIDTH)), -4.0, 4.0)
    return (base * row_scale * col_scale).astype(jnp.float32).astype(jnp.bfloat16)


def head_gain(key, salt):
    key = jax.random.fold_in(key, salt)
    values = jax.random.uniform(key, (HEAD_SIZE,), minval=0.5, maxval=2.0)
    return values.astype(jnp.float32).astype(jnp.bfloat16)


def draw_query_gain(key, part):
    return head_gain(key, 17)


def draw_key_gain(key, part):
    return head_gain(key, 29)


def draw_lengths(key, part):
    key = jax.random.fold_in(key, 11)

    def one_batch(batch_key):
        cut_key, order_key = jax.random.split(batch_key)
        longest_pages = PAGES_PER_BATCH // 2
        spare = PAGES_PER_BATCH - longest_pages - (NPROMPT - 1)
        cuts = jnp.sort(jax.random.randint(cut_key, (NPROMPT - 2,), 0, spare + 1))
        edges = jnp.concatenate([jnp.zeros((1,), jnp.int32), cuts.astype(jnp.int32), jnp.full((1,), spare, jnp.int32)])
        others = edges[1:] - edges[:-1] + 1
        counts = jnp.concatenate([jnp.full((1,), longest_pages, jnp.int32), others])
        return (jax.random.permutation(order_key, counts) * PAGE_TOKENS).astype(jnp.int32)
    return jax.vmap(one_batch)(jax.random.split(key, BATCH_COUNT))


def draw_page_table(key, part):
    key = jax.random.fold_in(key, 23)
    order_key, slot_key = jax.random.split(key)
    orders = jax.vmap(lambda one_key: jax.random.permutation(one_key, PAGES_PER_BATCH))(jax.random.split(order_key, BATCH_COUNT)).astype(jnp.int32)
    owner_slots = jax.vmap(lambda one_key: jax.random.permutation(one_key, PAGES_PER_BATCH))(jax.random.split(slot_key, BATCH_COUNT)).astype(jnp.int32)
    position = jnp.arange(PAGES_PER_BATCH, dtype=jnp.int32)
    owners = position // CAPP
    within = position % CAPP
    sources = jnp.arange(BATCH_COUNT, dtype=jnp.int32)[:, None]
    dest = owners[None, :] * PAGES_PER_BATCH + owner_slots[owners[None, :], sources * CAPP + within[None, :]]
    table = jnp.zeros((BATCH_COUNT, PAGES_PER_BATCH), jnp.int32).at[jnp.broadcast_to(sources, (BATCH_COUNT, PAGES_PER_BATCH)), orders].set(dest.astype(jnp.int32))
    return table.reshape(BATCH_COUNT * PAGES_PER_BATCH)


def with_ends(array, rng, smallest, top_value):
    dims = array.shape
    place = [jax.random.randint(jax.random.fold_in(rng, axis), (), 0, dims[axis]) for axis in range(len(dims))]
    array = array.at[tuple(place)].set(smallest)
    longest = dims.index(max(dims))
    place[longest] = (place[longest] + 1) % dims[longest]
    return array.at[tuple(place)].set(top_value)


def block_levels(rng, extent, pieces, least, top_value):
    factor_of, own = 1.0, jax.random.fold_in(rng, 6)
    for dim, blocks in pieces:
        heights = jnp.exp(jax.random.uniform(jax.random.fold_in(own, dim), (blocks,), jnp.float32, least / len(pieces), top_value / len(pieces)))
        factor_of = factor_of * jnp.repeat(heights, extent[dim] // blocks).reshape([-1 if axis == dim else 1 for axis in range(len(extent))])
    return factor_of


def centred(rng, shape, width, bound, cuts=(), kind=jnp.bfloat16):
    level = block_levels(rng, shape, cuts, -0.22, 0.18) if cuts else 1.0
    array = jax.random.normal(rng, shape, jnp.float32) * width * level
    return jnp.minimum(jnp.maximum(array, -bound), bound).astype(kind)


def setup_inputs(seed: int = 0) -> dict:
    streams_of = jax.random.split(jax.random.key(seed), 15)
    return {
        "stream": draw_stream(jax.random.fold_in(streams_of[14], 71), 0),
        "lengths": draw_lengths(jax.random.fold_in(streams_of[14], 71), 0),
        "page_table": draw_page_table(jax.random.fold_in(streams_of[14], 71), 0),
        "request_prompt": with_ends(jax.random.randint(streams_of[3], (BATCH_COUNT * NREQ,), 0, BATCH_COUNT * NPROMPT), jax.random.fold_in(streams_of[3], 1), 0, (BATCH_COUNT * NPROMPT) - 1).astype(jnp.int32),
        "attn_gain": jnp.clip(1.0 + 0.18 * jax.random.normal(streams_of[4], (MODEL_WIDTH,), jnp.float32), 0.099609375, 1.8984375).astype(jnp.bfloat16),
        "query_gain": draw_query_gain(jax.random.fold_in(streams_of[14], 71), 0),
        "key_gain": draw_key_gain(jax.random.fold_in(streams_of[14], 71), 0),
        "mlp_gain": jnp.clip(1.0 + 0.18 * jax.random.normal(streams_of[7], (MODEL_WIDTH,), jnp.float32), 0.099609375, 1.8984375).astype(jnp.bfloat16),
        "w_query": centred(streams_of[8], (MODEL_WIDTH, QUERY_HEADS * HEAD_SIZE), MODEL_WIDTH ** -0.5, 0.125, ((1, 8),)),
        "key_value_weight": centred(streams_of[9], (MODEL_WIDTH, 2 * KEY_VALUE_HEADS * HEAD_SIZE), MODEL_WIDTH ** -0.5, 0.125, ((1, 8),)),
        "w_out": centred(streams_of[10], (QUERY_HEADS * HEAD_SIZE, MODEL_WIDTH), HEAD_SIZE ** -0.5, 0.5, ((0, 8),)),
        "w_gate": centred(streams_of[11], (MODEL_WIDTH, FF), MODEL_WIDTH ** -0.5, 0.125, ((1, 8),)),
        "w_up": centred(streams_of[12], (MODEL_WIDTH, FF), MODEL_WIDTH ** -0.5, 0.125, ((1, 8),)),
        "w_down": centred(streams_of[13], (FF, MODEL_WIDTH), FF ** -0.5, 0.0625, ((0, 8),)),
    }


epsilon = 1e-06
rope_base = 1000000.0

def row_norm(inputs, gain):
    inputs = inputs.astype(jnp.float32)
    scale = lax.rsqrt(lax.optimization_barrier(jnp.mean(inputs * inputs, axis=-1, keepdims=True)) + epsilon)
    return inputs * scale * gain.astype(jnp.float32)

def rotate(inputs, position):
    half_dim = inputs.shape[-1] // 2
    frequency = rope_base ** (-2.0 * jnp.arange(half_dim, dtype=jnp.float32) / inputs.shape[-1])
    angles = position.astype(jnp.float32)[:, None] * frequency[None, :]
    cosine = jnp.cos(angles)[:, None, :]
    sine_part = jnp.sin(angles)[:, None, :]
    front = inputs[..., :half_dim]
    second = inputs[..., half_dim:]
    return jnp.concatenate([front * cosine - second * sine_part, second * cosine + front * sine_part], axis=-1)

def prompt_layout(lengths_row, token_count):
    lengths_row = lengths_row.astype(jnp.int32)
    prompt_ends = jnp.cumsum(lengths_row).astype(jnp.int32)
    prompt_starts = (prompt_ends - lengths_row).astype(jnp.int32)
    row_ids = jnp.arange(token_count, dtype=jnp.int32)
    prompt = lax.optimization_barrier(jnp.sum((row_ids[:, None] >= prompt_ends[None, :]).astype(jnp.int32), axis=1)).astype(jnp.int32)
    inside = (row_ids[:, None] >= prompt_starts[None, :]) & (row_ids[:, None] < prompt_ends[None, :])
    offset = lax.optimization_barrier(jnp.sum(jnp.where(inside, prompt_starts[None, :], 0), axis=1)).astype(jnp.int32)
    return (prompt, (row_ids - offset).astype(jnp.int32), prompt_starts, prompt_ends)

def block_sum(left, right, block_count):
    width_block = left.shape[1] // block_count

    def add_block(block_id, summed):
        portion = lax.dynamic_slice_in_dim(left, block_id * width_block, width_block, 1)
        weights = lax.dynamic_slice_in_dim(right, block_id * width_block, width_block, 0)
        partial_value = jnp.dot(portion, weights, preferred_element_type=jnp.float32).astype(jnp.bfloat16)
        partial_value = lax.optimization_barrier(partial_value)
        return summed + partial_value.astype(jnp.float32)
    start_sum = jnp.zeros((left.shape[0], right.shape[1]), jnp.float32)
    return lax.fori_loop(jnp.int32(0), jnp.int32(block_count), add_block, start_sum)

def reference(stream, lengths, page_table, request_prompt, attn_gain, query_gain, key_gain, mlp_gain, w_query, key_value_weight, w_out, w_gate, w_up, w_down):
    queries_per_key_value = QUERY_HEADS // KEY_VALUE_HEADS
    outputs = []
    last_rows = []
    paged_key_value_cache = jnp.zeros((BATCH_COUNT * PAGES_PER_BATCH, PAGE_TOKENS, 2 * KEY_VALUE_HEADS * HEAD_SIZE), jnp.bfloat16)
    token_ids = jnp.arange(BATCH_TOKENS, dtype=jnp.int32)
    for group_id in range(BATCH_COUNT):
        rows_in = stream[group_id * BATCH_TOKENS:(group_id + 1) * BATCH_TOKENS]
        prompt, position, prompt_starts, prompt_ends = prompt_layout(lengths[group_id], BATCH_TOKENS)
        normalized_rows = row_norm(rows_in, attn_gain).astype(jnp.bfloat16)
        queries = jnp.dot(normalized_rows, w_query, preferred_element_type=jnp.float32).reshape(BATCH_TOKENS, QUERY_HEADS, HEAD_SIZE)
        key_value_rows = jnp.dot(normalized_rows, key_value_weight, preferred_element_type=jnp.float32).astype(jnp.bfloat16).reshape(BATCH_TOKENS, KEY_VALUE_HEADS, 2, HEAD_SIZE)
        q_rot = rotate(row_norm(queries, query_gain), position).astype(jnp.bfloat16)
        rotated_key = rotate(row_norm(key_value_rows[:, :, 0, :], key_gain), position).astype(jnp.bfloat16)
        value_matrix_rows = key_value_rows[:, :, 1, :]
        allowed = (prompt[:, None] == prompt[None, :]) & (token_ids[:, None] >= token_ids[None, :])
        heads_out = []
        for key_value_head in range(KEY_VALUE_HEADS):
            q_group = q_rot[:, key_value_head * queries_per_key_value:(key_value_head + 1) * queries_per_key_value, :].astype(jnp.float32)
            key_head = rotated_key[:, key_value_head, :].astype(jnp.float32)
            scores = jnp.einsum('qhd,kd->hqk', q_group, key_head, precision=lax.Precision.HIGHEST) / math.sqrt(HEAD_SIZE)
            peak = lax.optimization_barrier(jnp.max(jnp.where(allowed[None], scores, -jnp.inf), axis=2, keepdims=True))
            weight = jnp.where(allowed[None], jnp.exp(scores - peak), 0.0)
            total_weight = lax.optimization_barrier(jnp.sum(weight, axis=2, keepdims=True))
            probs = lax.optimization_barrier(weight.astype(jnp.bfloat16)).astype(jnp.float32)
            mixed = jnp.einsum('hqk,kd->qhd', probs, value_matrix_rows[:, key_value_head, :].astype(jnp.float32), precision=lax.Precision.HIGHEST)
            heads_out.append((mixed / jnp.transpose(total_weight, (1, 0, 2))).astype(jnp.bfloat16))
        attn = jnp.concatenate(heads_out, axis=1).reshape(BATCH_TOKENS, QUERY_HEADS * HEAD_SIZE)
        attn_sum = block_sum(attn, w_out, N_TENSOR)
        resid = (rows_in.astype(jnp.float32) + attn_sum).astype(jnp.bfloat16)
        mlp_normed = row_norm(resid, mlp_gain).astype(jnp.bfloat16)
        gate_rows = jnp.dot(mlp_normed, w_gate, preferred_element_type=jnp.float32)
        upward = jnp.dot(mlp_normed, w_up, preferred_element_type=jnp.float32)
        hidden = (jax.nn.silu(gate_rows) * upward).astype(jnp.bfloat16)
        mlp_sum = block_sum(hidden, w_down, N_TENSOR)
        layer_rows = (resid.astype(jnp.float32) + mlp_sum).astype(jnp.bfloat16)
        outputs.append(layer_rows)
        cache_pages = jnp.stack([rotated_key, value_matrix_rows], axis=2).reshape(PAGES_PER_BATCH, PAGE_TOKENS, 2 * KEY_VALUE_HEADS * HEAD_SIZE)
        paged_key_value_cache = paged_key_value_cache.at[page_table[group_id * PAGES_PER_BATCH:(group_id + 1) * PAGES_PER_BATCH]].set(cache_pages)
        last_rows.append(layer_rows[prompt_ends - 1])
    layer_out = jnp.concatenate(outputs, axis=0)
    table = jnp.concatenate(last_rows, axis=0)
    request_state = table[request_prompt]
    return (layer_out, paged_key_value_cache, request_state)
```

```python
import math

import jax
import jax.numpy as jnp
from jax import lax
from jax.experimental import pallas as pl
from jax.experimental.pallas import tpu as pltpu
from jax.sharding import PartitionSpec as P

KEY_VALUE_HEADS = 8
HEAD_SIZE = 128
PAGE_TOKENS = 16
MESH = pl.DeviceIdType.MESH


epsilon = 1e-06
rope_base = 1000000.0


def partner_2(value, axis, bit):
    mask = 2**bit
    pairs = [(source, source ^ mask) for source in range(lax.axis_size(axis))]
    return lax.ppermute(value, axis, pairs)


def row_norm(inputs, gain):
    inputs = inputs.astype(jnp.float32)
    scale = lax.rsqrt(jnp.mean(inputs * inputs, axis=-1, keepdims=True) + epsilon)
    return inputs * scale * gain.astype(jnp.float32)


def rotate(inputs, position):
    half_dim = inputs.shape[-1] // 2
    frequency = rope_base ** (-2.0 * jnp.arange(half_dim, dtype=jnp.float32) / inputs.shape[-1])
    angles = position.astype(jnp.float32)[:, None] * frequency[None, :]
    cosine = jnp.cos(angles)[:, None, :]
    sine_part = jnp.sin(angles)[:, None, :]
    front = inputs[..., :half_dim]
    second = inputs[..., half_dim:]
    return jnp.concatenate(
        [front * cosine - second * sine_part, second * cosine + front * sine_part], axis=-1
    )


def prompt_layout(lengths_row, token_count):
    prompt_ends = jnp.cumsum(lengths_row)
    prompt_starts = prompt_ends - lengths_row
    row_ids = jnp.arange(token_count, dtype=jnp.int32)
    prompt = jnp.sum((row_ids[:, None] >= prompt_ends[None, :]).astype(jnp.int32), axis=1)
    inside = (row_ids[:, None] >= prompt_starts[None, :]) & (
        row_ids[:, None] < prompt_ends[None, :]
    )
    offset = jnp.sum(jnp.where(inside, prompt_starts[None, :], 0), axis=1)
    return (prompt, row_ids - offset, prompt_starts, prompt_ends)


def per_device(
    stream,
    lengths,
    page_table,
    request_prompt,
    attn_gain,
    query_gain,
    key_gain,
    mlp_gain,
    w_query,
    key_value_weight,
    w_out,
    w_gate,
    w_up,
    w_down,
):
    tok_dev = stream.shape[0]
    tensor_element_count = lax.axis_size("tensor")
    token_count = tok_dev * tensor_element_count
    my_index = lax.axis_index("tensor")
    heads_dev = w_query.shape[1] // HEAD_SIZE
    query_cols = heads_dev * HEAD_SIZE
    prompt, position, prompt_starts, prompt_ends = prompt_layout(lengths[0], token_count)
    portion = lax.all_gather(
        row_norm(stream, attn_gain).astype(jnp.bfloat16), "tensor", axis=0, tiled=True
    )
    joined = jnp.concatenate(
        [
            jnp.dot(portion, w_query, preferred_element_type=jnp.float32),
            jnp.dot(portion, key_value_weight, preferred_element_type=jnp.float32),
        ],
        axis=1,
    )
    queries = joined[:, :query_cols].reshape(token_count, heads_dev, HEAD_SIZE)
    kv_part = joined[:, query_cols:].astype(jnp.bfloat16)
    key_value_group = tensor_element_count // KEY_VALUE_HEADS
    for bit_id in range(key_value_group.bit_length() - 1):
        partner = partner_2(kv_part, "tensor", bit_id)
        upper_half = my_index // 2**bit_id % 2
        kv_part = jnp.where(
            upper_half == 1,
            jnp.concatenate([partner, kv_part], axis=1),
            jnp.concatenate([kv_part, partner], axis=1),
        )
    key_flat = rotate(row_norm(kv_part[:, None, :HEAD_SIZE], key_gain), position).astype(
        jnp.bfloat16
    )[:, 0, :]
    value_matrix_rows = kv_part[:, HEAD_SIZE:]
    q_rot = rotate(row_norm(queries, query_gain), position).astype(jnp.bfloat16)
    piece_cols = key_value_weight.shape[1]
    head_rows = jnp.concatenate([key_flat, value_matrix_rows], axis=1)
    own_cols = lax.dynamic_slice_in_dim(
        head_rows, my_index % key_value_group * piece_cols, piece_cols, 1
    )
    page_count = token_count // PAGE_TOKENS
    page_rows = own_cols.reshape(page_count, PAGE_TOKENS, piece_cols)
    group_count = lax.axis_size("dp")
    capacity = page_count // group_count
    owners = page_table // page_count
    slot_ids = page_table % page_count
    hits = (owners[:, None] == jnp.arange(group_count, dtype=jnp.int32)[None, :]).astype(jnp.int32)
    order_in = jnp.sum((jnp.cumsum(hits, axis=0) - hits) * hits, axis=1)
    buffer_pos = owners * capacity + order_in
    source = (
        jnp.zeros((page_count,), jnp.int32)
        .at[buffer_pos]
        .set(jnp.arange(page_count, dtype=jnp.int32))
    )
    send_pages = page_rows[source].reshape(group_count, capacity, PAGE_TOKENS, piece_cols)
    send_slots = slot_ids[source].reshape(group_count, capacity)
    got_pages, got_slots = (
        lax.all_to_all(send_pages, "dp", split_axis=0, concat_axis=0, tiled=True),
        lax.all_to_all(send_slots, "dp", split_axis=0, concat_axis=0, tiled=True),
    )
    paged_key_value_cache = (
        jnp.zeros((page_count, PAGE_TOKENS, piece_cols), jnp.bfloat16)
        .at[got_slots.reshape(-1)]
        .set(got_pages.reshape(page_count, PAGE_TOKENS, piece_cols))
    )
    block_rows = min(512, token_count)
    block_total = token_count // block_rows
    score_scale = math.sqrt(HEAD_SIZE)
    all_ids = jnp.arange(token_count, dtype=jnp.int32)
    local_ids = jnp.arange(block_rows, dtype=jnp.int32)

    def dense_block(block_index):
        first_row = block_index * block_rows
        q_block = lax.dynamic_slice_in_dim(q_rot, first_row, block_rows, 0)
        q_prompt = lax.dynamic_slice_in_dim(prompt, first_row, block_rows, 0)
        row_ids = first_row + local_ids
        scores = (
            jnp.einsum("qhd,kd->hqk", q_block, key_flat, preferred_element_type=jnp.float32)
            / score_scale
        )
        allowed = ((q_prompt[:, None] == prompt[None, :]) & (row_ids[:, None] >= all_ids[None, :]))[
            None
        ]
        peak = jnp.max(jnp.where(allowed, scores, -jnp.inf), axis=2, keepdims=True)
        weight = jnp.where(allowed, jnp.exp(scores - peak), 0.0)
        total_weight = jnp.sum(weight, axis=2, keepdims=True)
        running = jnp.einsum(
            "hqk,kd->hqd",
            weight.astype(jnp.bfloat16),
            value_matrix_rows,
            preferred_element_type=jnp.float32,
        )
        return (running / total_weight).astype(jnp.bfloat16)

    block_ids = jnp.arange(block_total, dtype=jnp.int32)
    blocks_out = lax.map(dense_block, block_ids)
    attn = jnp.transpose(blocks_out, (0, 2, 1, 3)).reshape(token_count, query_cols)
    attn_sum = lax.psum_scatter(
        jnp.dot(attn, w_out, preferred_element_type=jnp.float32).astype(jnp.bfloat16),
        "tensor",
        scatter_dimension=0,
        tiled=True,
    ).astype(jnp.float32)
    resid = (stream.astype(jnp.float32) + attn_sum).astype(jnp.bfloat16)
    portion = lax.all_gather(
        row_norm(resid, mlp_gain).astype(jnp.bfloat16), "tensor", axis=0, tiled=True
    )
    gate_rows = jnp.dot(portion, w_gate, preferred_element_type=jnp.float32)
    upward = jnp.dot(portion, w_up, preferred_element_type=jnp.float32)
    hidden = (jax.nn.silu(gate_rows) * upward).astype(jnp.bfloat16)
    mlp_sum = lax.psum_scatter(
        jnp.dot(hidden, w_down, preferred_element_type=jnp.float32).astype(jnp.bfloat16),
        "tensor",
        scatter_dimension=0,
        tiled=True,
    ).astype(jnp.float32)
    layer_out = (resid.astype(jnp.float32) + mlp_sum).astype(jnp.bfloat16)
    my_rows = my_index * tok_dev + jnp.arange(tok_dev, dtype=jnp.int32)
    select = ((prompt_ends - 1)[:, None] == my_rows[None, :]).astype(jnp.bfloat16)
    end_terms = jnp.dot(select, layer_out, preferred_element_type=jnp.float32)
    end_rows = lax.psum_scatter(
        end_terms.astype(jnp.bfloat16), "tensor", scatter_dimension=1, tiled=True
    )
    table = lax.all_gather(end_rows, "dp", axis=0, tiled=True)
    pick = (request_prompt[:, None] == jnp.arange(table.shape[0], dtype=jnp.int32)[None, :]).astype(
        jnp.bfloat16
    )
    request_state = jnp.dot(pick, table, preferred_element_type=jnp.float32).astype(jnp.bfloat16)
    return (layer_out, paged_key_value_cache, request_state)


def fused_kernel(
    lengths_ref,
    stream_ref,
    slots_ref,
    request_ref,
    attn_gain_ref,
    query_gain_ref,
    key_gain_ref,
    mlp_gain_ref,
    frequency_ref,
    wq_hbm,
    wkv_hbm,
    wo_hbm,
    wg_hbm,
    wu_hbm,
    wd_hbm,
    layer_ref,
    cache_ref,
    state_ref,
    wq,
    wkv,
    wo,
    wg,
    wu,
    wd,
    gathered,
    q_rot,
    kv_all,
    slots_all,
    attn,
    hidden,
    part,
    y_in,
    z_out,
    z_in,
    cosine,
    sine,
    starts,
    resid,
    end_out,
    end_in,
    table,
    weight_sem,
    ag_recv,
    ag_zsend,
    ag_ysend,
    rs_yrecv,
    rs_ysend,
    rs_zrecv,
    rs_zsend,
    kv_send,
    kv_recv,
    slots_send,
    slots_recv,
    end_send,
    end_recv,
    table_send,
    table_recv,
):
    f32 = jnp.float32
    bf16 = jnp.bfloat16
    t = lax.axis_index("tensor")
    g = lax.axis_index("dp")
    z = t // 2
    y = t % 2
    rows = stream_ref.shape[0]
    width = stream_ref.shape[1]
    tokens = rows * 8

    pairs = ((wq_hbm, wq), (wkv_hbm, wkv), (wo_hbm, wo), (wg_hbm, wg), (wu_hbm, wu), (wd_hbm, wd))
    loads = [
        pltpu.make_async_copy(source, target, weight_sem.at[k])
        for k, (source, target) in enumerate(pairs)
    ]
    for load in loads:
        load.start()

    barrier = pltpu.get_barrier_semaphore()
    for k in range(1, 8):
        pl.semaphore_signal(barrier, inc=1, device_id=(g, (t + k) % 8), device_id_type=MESH)
    for k in range(1, 4):
        pl.semaphore_signal(barrier, inc=1, device_id=((g + k) % 4, t), device_id_type=MESH)

    def normed(value, gain_ref):
        scale = lax.rsqrt(jnp.mean(value * value, axis=-1, keepdims=True) + epsilon)
        return value * scale * gain_ref[...].astype(f32)

    gathered[0, t] = normed(stream_ref[...].astype(f32), attn_gain_ref).astype(bf16)
    pl.semaphore_wait(barrier, 10)

    def y_copy(source, target, send, recv):
        return pltpu.make_async_remote_copy(
            src_ref=source, dst_ref=target, send_sem=send, recv_sem=recv,
            device_id=(g, z * 2 + 1 - y), device_id_type=MESH)

    def z_copy(source, target, send, recv, step):
        return pltpu.make_async_remote_copy(
            src_ref=source, dst_ref=target, send_sem=send, recv_sem=recv,
            device_id=(g, (z + step) * 2 + y), device_id_type=MESH)

    def gather(phase, before, process):
        def up(s):
            slot = (z - s) * 2 + y
            return z_copy(gathered.at[phase, slot], gathered.at[phase, slot],
                          ag_zsend.at[phase, 0, s], ag_recv.at[phase, slot], 1)

        def down(s):
            slot = (z + s) * 2 + y
            return z_copy(gathered.at[phase, slot], gathered.at[phase, slot],
                          ag_zsend.at[phase, 1, s], ag_recv.at[phase, slot], -1)

        def across(level):
            slot = level * 2 + y
            return y_copy(gathered.at[phase, slot], gathered.at[phase, slot],
                          ag_ysend.at[phase, level], ag_recv.at[phase, slot])

        def arrived(slot):
            y_copy(gathered.at[phase, slot], gathered.at[phase, slot],
                   ag_ysend.at[phase, 0], ag_recv.at[phase, slot]).wait_recv()

        def group(level):
            arrived(level * 2 + 1 - y)
            process(level)

        def groups(s):
            if s == 0:
                group(z)
            else:
                pl.when(z - s >= 0)(lambda: group(z - s))
                pl.when(z + s <= 3)(lambda: group(z + s))

        for s in range(4):
            if s:
                @pl.when(z - s >= 0)
                def _():
                    arrived((z - s) * 2 + y)

                    @pl.when(z < 3)
                    def _():
                        up(s).start()

                    across(z - s).start()

                @pl.when(z + s <= 3)
                def _():
                    arrived((z + s) * 2 + y)

                    @pl.when(z > 0)
                    def _():
                        down(s).start()

                    across(z + s).start()

                groups(s - 1)
            else:
                pl.when(z < 3)(lambda: up(0).start())
                pl.when(z > 0)(lambda: down(0).start())
                across(z).start()
                before()
        groups(3)

        for s in range(4):
            pl.when((z - s >= 0) & (z < 3))(lambda: up(s).wait_send())
            pl.when((z + s <= 3) & (z > 0))(lambda: down(s).wait_send())
            across(s).wait_send()

    packed = 27 + 72 * z - 15 * (z * (z - 1) // 2) + 5 * (z * (z - 1) * (z - 2))
    order = [packed % 4, packed // 4 % 4, packed // 16 % 4, packed // 64]

    def send_part(phase, level):
        return y_copy(part.at[phase, level, 1 - y], y_in.at[phase, level],
                      rs_ysend.at[phase, level], rs_yrecv.at[phase, level])

    def flow(phase, level, direction, step):
        return z_copy(z_out.at[phase, level], z_in.at[phase, direction, level],
                      rs_zsend.at[phase, level], rs_zrecv.at[phase, direction, level], step)

    def scatter(phase):
        for i in range(3):
            level = order[i]
            send_part(phase, level).wait_recv()

            @pl.when(level > z)
            def _():
                total = part[phase, level, y].astype(f32) + y_in[phase, level].astype(f32)

                @pl.when(z > 0)
                def _():
                    flow(phase, level, 0, 1).wait_recv()
                    z_out[phase, level] = (total + z_in[phase, 0, level].astype(f32)).astype(bf16)

                @pl.when(z == 0)
                def _():
                    z_out[phase, level] = total.astype(bf16)

                flow(phase, level, 0, 1).start()

            @pl.when(level < z)
            def _():
                total = part[phase, level, y].astype(f32) + y_in[phase, level].astype(f32)

                @pl.when(z < 3)
                def _():
                    flow(phase, level, 1, -1).wait_recv()
                    z_out[phase, level] = (total + z_in[phase, 1, level].astype(f32)).astype(bf16)

                @pl.when(z == 3)
                def _():
                    z_out[phase, level] = total.astype(bf16)

                flow(phase, level, 1, -1).start()

        send_part(phase, z).wait_recv()
        resid[1] = part[phase, z, y].astype(f32) + y_in[phase, z].astype(f32)

        @pl.when(z > 0)
        def _():
            flow(phase, z, 0, 1).wait_recv()
            resid[1] = resid[1] + z_in[phase, 0, z].astype(f32)

        @pl.when(z < 3)
        def _():
            flow(phase, z, 1, -1).wait_recv()
            resid[1] = resid[1] + z_in[phase, 1, z].astype(f32)

        for level in range(4):
            send_part(phase, level).wait_send()
            pl.when(z != level)(lambda: flow(phase, level, 0, 1).wait_send())
        return resid[1]

    def angles():
        ids = lax.broadcasted_iota(jnp.int32, (tokens, HEAD_SIZE), 0)
        begin = jnp.int32(0)
        offset = jnp.zeros((tokens, HEAD_SIZE), jnp.int32)
        for k in range(lengths_ref.shape[1]):
            end = begin + lengths_ref[0, k]
            offset = jnp.where((ids >= begin) & (ids < end), begin, offset)
            begin = end
        starts[...] = offset
        angle = (ids - offset).astype(f32) * frequency_ref[...]
        lane = lax.broadcasted_iota(jnp.int32, (tokens, HEAD_SIZE), 1)
        cosine[...] = jnp.cos(angle)
        signed = jnp.sin(angle)
        sine[...] = jnp.where(lane < HEAD_SIZE // 2, -signed, signed)
        slots_all[0] = slots_ref[...]
        loads[0].wait()
        loads[1].wait()

    heads = wq.shape[1] // HEAD_SIZE

    def project(level):
        inputs = gathered[0, pl.ds(level * 2, 2)].reshape(2 * rows, width)
        span = pl.ds(pl.multiple_of(level * 2 * rows, 32), 2 * rows)
        cos_rows = cosine[span, :]
        sin_rows = sine[span, :]

        def rotated(value):
            return value * cos_rows + pltpu.roll(value, HEAD_SIZE // 2, 1) * sin_rows

        for pair in range(heads // 2):
            block = jnp.dot(inputs, wq[:, pair * 256:(pair + 1) * 256], preferred_element_type=f32)
            for k in range(2):
                head = block[:, k * HEAD_SIZE:(k + 1) * HEAD_SIZE]
                q_rot[pair * 2 + k, span, :] = rotated(normed(head, query_gain_ref)).astype(bf16)
        keyval = jnp.dot(inputs, wkv[...], preferred_element_type=f32).astype(bf16)
        key_head = keyval[:, :HEAD_SIZE].astype(f32)
        kv_all[0, span, :HEAD_SIZE] = rotated(normed(key_head, key_gain_ref)).astype(bf16)
        kv_all[0, span, HEAD_SIZE:] = keyval[:, HEAD_SIZE:]

    gather(0, angles, project)

    def kv_copies(k):
        peer = (lax.rem(g + k, 4), t)
        return (
            pltpu.make_async_remote_copy(
                src_ref=kv_all.at[0], dst_ref=kv_all.at[k], send_sem=kv_send.at[k],
                recv_sem=kv_recv.at[k], device_id=peer, device_id_type=MESH),
            pltpu.make_async_remote_copy(
                src_ref=slots_all.at[0], dst_ref=slots_all.at[k], send_sem=slots_send.at[k],
                recv_sem=slots_recv.at[k], device_id=peer, device_id_type=MESH),
        )

    for k in range(1, 4):
        for copy in kv_copies(k):
            copy.start()

    block = 128
    for q_block in range(tokens // block):
        span = q_block * block
        keys = span + block
        row_id = span + lax.broadcasted_iota(jnp.int32, (block, keys), 0)
        key_id = lax.broadcasted_iota(jnp.int32, (block, keys), 1)
        first = jnp.concatenate([starts[span:keys, :]] * (keys // block), axis=1)
        allowed = (key_id >= first) & (key_id <= row_id)
        key_rows = kv_all[0, :keys, :HEAD_SIZE]
        value_rows = kv_all[0, :keys, HEAD_SIZE:]
        for head in range(heads):
            scores = lax.dot_general(
                q_rot[head, span:keys, :], key_rows, (((1,), (1,)), ((), ())),
                preferred_element_type=f32) * (1.0 / math.sqrt(HEAD_SIZE))
            scores = jnp.where(allowed, scores, -jnp.inf)
            peak = jnp.max(scores, axis=1, keepdims=True)
            weight = jnp.exp(scores - peak)
            total_weight = jnp.sum(weight, axis=1, keepdims=True)
            mixed = jnp.dot(weight.astype(bf16), value_rows, preferred_element_type=f32)
            attn[span:keys, head * HEAD_SIZE:(head + 1) * HEAD_SIZE] = (
                mixed / total_weight).astype(bf16)

    tile = 256

    loads[2].wait()
    for i in range(4):
        level = order[i]
        span = pl.ds(pl.multiple_of(level * 2 * rows, 32), 2 * rows)
        inputs = attn[span, :]

        @pl.loop(0, width // tile)
        def _(n):
            cols = pl.ds(pl.multiple_of(n * tile, tile), tile)
            out = jnp.dot(inputs, wo[:, cols], preferred_element_type=f32)
            part[0, level, :, :, cols] = out.astype(bf16).reshape(2, rows, tile)

        send_part(0, level).start()

    attn_sum = scatter(0)
    residual = (stream_ref[...].astype(f32) + attn_sum).astype(bf16)
    resid[0] = residual.astype(f32)
    gathered[1, t] = normed(resid[0], mlp_gain_ref).astype(bf16)

    def fill_cache():
        row = g * tokens + lax.broadcasted_iota(jnp.int32, (tokens, tokens), 0)
        total = None
        for k in range(4):
            if k:
                for copy in kv_copies(k):
                    copy.wait()
            pick = (slots_all[k, 0:1, :] == row).astype(f32).astype(bf16)
            term = jnp.dot(pick, kv_all[k], preferred_element_type=f32)
            total = term if total is None else total + term
        cache_ref[...] = total.astype(bf16)
        loads[3].wait()
        loads[4].wait()
        loads[5].wait()

    hidden_width = wg.shape[1]

    def feed_forward(level):
        inputs = gathered[1, pl.ds(level * 2, 2)].reshape(2 * rows, width)
        for start in range(0, hidden_width, tile):
            stop = min(start + tile, hidden_width)
            gate = jnp.dot(inputs, wg[:, start:stop], preferred_element_type=f32)
            upward = jnp.dot(inputs, wu[:, start:stop], preferred_element_type=f32)
            hidden[:, start:stop] = (gate / (1.0 + jnp.exp(-gate)) * upward).astype(bf16)
        inner = hidden[...]

        @pl.loop(0, width // tile)
        def _(n):
            cols = pl.ds(pl.multiple_of(n * tile, tile), tile)
            out = jnp.dot(inner, wd[:, cols], preferred_element_type=f32)
            part[1, level, :, :, cols] = out.astype(bf16).reshape(2, rows, tile)

        send_part(1, level).start()

    gather(1, fill_cache, feed_forward)
    mlp_sum = scatter(1)
    layer_out = (resid[0] + mlp_sum).astype(bf16)
    layer_ref[...] = layer_out

    slots = end_out.shape[1]
    span_cols = end_out.shape[2]
    row_id = t * rows + lax.broadcasted_iota(jnp.int32, (slots, rows), 1)
    slot_id = lax.broadcasted_iota(jnp.int32, (slots, rows), 0)
    end = jnp.int32(0)
    hit = jnp.zeros((slots, rows), f32)
    for k in range(lengths_ref.shape[1]):
        end = end + lengths_ref[0, k]
        hit = jnp.where((slot_id == k) & (row_id == end - 1), 1.0, hit)
    terms = jnp.dot(hit.astype(bf16), layer_out, preferred_element_type=f32).astype(bf16)
    for k in range(8):
        first = k * 5 // 2 * 128
        end_out[k] = terms[:, first:first + span_cols]

    def end_copy(k):
        peer = lax.rem(t + k, 8)
        return pltpu.make_async_remote_copy(
            src_ref=end_out.at[peer], dst_ref=end_in.at[k], send_sem=end_send.at[k],
            recv_sem=end_recv.at[k], device_id=(g, peer), device_id_type=MESH)

    for k in range(1, 8):
        end_copy(k).start()
    total = end_out[t].astype(f32)
    for k in range(1, 8):
        end_copy(k).wait()
        total = total + end_in[k].astype(f32)
    table[0] = total.astype(bf16)

    def table_copy(k):
        return pltpu.make_async_remote_copy(
            src_ref=table.at[0], dst_ref=table.at[k], send_sem=table_send.at[k],
            recv_sem=table_recv.at[k], device_id=(lax.rem(g + k, 4), t), device_id_type=MESH)

    for k in range(1, 4):
        table_copy(k).start()
    prompts = lengths_ref.shape[1]
    asked = request_ref[:, :slots]
    column = lax.broadcasted_iota(jnp.int32, (asked.shape[0], slots), 1)
    state = None
    for k in range(4):
        if k:
            table_copy(k).wait()
        batch = lax.rem(g + 4 - k, 4)
        pick = ((asked == batch * prompts + column) & (column < prompts)).astype(f32).astype(bf16)
        term = jnp.dot(pick, table[k], preferred_element_type=f32)
        state = term if state is None else state + term
    keep = state_ref.shape[1]
    shifted = state[:, span_cols - keep:]
    state_ref[...] = jnp.where(t % 2 == 1, shifted, state[:, :keep]).astype(bf16)


def fused_device(
    stream,
    lengths,
    page_table,
    request_prompt,
    attn_gain,
    query_gain,
    key_gain,
    mlp_gain,
    w_query,
    key_value_weight,
    w_out,
    w_gate,
    w_up,
    w_down,
):
    rows, width = stream.shape
    tokens = rows * 8
    query_cols = w_query.shape[1]
    keyval_cols = key_value_weight.shape[1]
    hidden_width = w_gate.shape[1]
    heads = query_cols // HEAD_SIZE
    requests = request_prompt.shape[0]
    state_cols = width // 8
    half = HEAD_SIZE // 2
    frequency = rope_base ** (-2.0 * jnp.arange(half, dtype=jnp.float32) / HEAD_SIZE)
    frequency = jnp.concatenate([frequency, frequency])[None, :]
    cache_rows = page_table[:, None] * PAGE_TOKENS + jnp.arange(PAGE_TOKENS, dtype=jnp.int32)[None, :]
    slots = jnp.broadcast_to(cache_rows.reshape(1, tokens), (8, tokens))
    asked = jnp.broadcast_to(request_prompt[:, None], (requests, 128))
    bf16 = jnp.bfloat16
    f32 = jnp.float32
    vmem = pl.BlockSpec(memory_space=pltpu.VMEM)
    smem = pl.BlockSpec(memory_space=pltpu.SMEM)
    hbm = pl.BlockSpec(memory_space=pl.ANY)
    dma = pltpu.SemaphoreType.DMA
    layer_out, cache, state = pl.pallas_call(
        fused_kernel,
        out_shape=(
            jax.ShapeDtypeStruct((rows, width), bf16),
            jax.ShapeDtypeStruct((tokens, keyval_cols), bf16),
            jax.ShapeDtypeStruct((requests, state_cols), bf16),
        ),
        in_specs=[smem] + [vmem] * 8 + [hbm] * 6,
        out_specs=(vmem, vmem, vmem),
        scratch_shapes=[
            pltpu.VMEM((width, query_cols), bf16),
            pltpu.VMEM((width, keyval_cols), bf16),
            pltpu.VMEM((query_cols, width), bf16),
            pltpu.VMEM((width, hidden_width), bf16),
            pltpu.VMEM((width, hidden_width), bf16),
            pltpu.VMEM((hidden_width, width), bf16),
            pltpu.VMEM((2, 8, rows, width), bf16),
            pltpu.VMEM((heads, tokens, HEAD_SIZE), bf16),
            pltpu.VMEM((4, tokens, keyval_cols), bf16),
            pltpu.VMEM((4, 8, tokens), jnp.int32),
            pltpu.VMEM((tokens, query_cols), bf16),
            pltpu.VMEM((2 * rows, hidden_width), bf16),
            pltpu.VMEM((2, 4, 2, rows, width), bf16),
            pltpu.VMEM((2, 4, rows, width), bf16),
            pltpu.VMEM((2, 4, rows, width), bf16),
            pltpu.VMEM((2, 2, 4, rows, width), bf16),
            pltpu.VMEM((tokens, HEAD_SIZE), f32),
            pltpu.VMEM((tokens, HEAD_SIZE), f32),
            pltpu.VMEM((tokens, HEAD_SIZE), jnp.int32),
            pltpu.VMEM((2, rows, width), f32),
            pltpu.VMEM((8, 16, 384), bf16),
            pltpu.VMEM((8, 16, 384), bf16),
            pltpu.VMEM((4, 16, 384), bf16),
            dma((6,)),
            dma((2, 8)),
            dma((2, 2, 4)),
            dma((2, 4)),
            dma((2, 4)),
            dma((2, 4)),
            dma((2, 2, 4)),
            dma((2, 4)),
            dma((4,)),
            dma((4,)),
            dma((4,)),
            dma((4,)),
            dma((8,)),
            dma((8,)),
            dma((4,)),
            dma((4,)),
        ],
        compiler_params=pltpu.CompilerParams(
            collective_id=0, has_side_effects=True, vmem_limit_bytes=60 * 1024 * 1024
        ),
        name="fused_layer",
    )(
        lengths, stream, slots, asked, attn_gain[None, :], query_gain[None, :], key_gain[None, :],
        mlp_gain[None, :], frequency, w_query, key_value_weight, w_out, w_gate, w_up, w_down,
    )
    return layer_out, cache.reshape(tokens // PAGE_TOKENS, PAGE_TOKENS, keyval_cols), state


def solution(mesh):
    placed = (
        P(("dp", "tensor"), None),
        P("dp", None),
        P("dp"),
        P("dp"),
        P(),
        P(),
        P(),
        P(),
        P(None, "tensor"),
        P(None, "tensor"),
        P("tensor", None),
        P(None, "tensor"),
        P(None, "tensor"),
        P("tensor", None),
    )
    fused = mesh.shape["tensor"] == KEY_VALUE_HEADS and mesh.shape["dp"] == 4
    return jax.shard_map(
        fused_device if fused else per_device,
        mesh=mesh,
        in_specs=placed,
        out_specs=(P(("dp", "tensor"), None), P("dp", None, "tensor"), P("dp", "tensor")),
        check_vma=False,
    )
```

```python
import math

import jax
import jax.numpy as jnp
import numpy as np
from jax import lax
from jax.experimental import pallas as pl
from jax.experimental.pallas import tpu as pltpu
from jax.sharding import PartitionSpec as P

KEY_VALUE_HEADS = 8
HEAD_SIZE = 128
PAGE_TOKENS = 16
MESH = pl.DeviceIdType.MESH


epsilon = 1e-06
rope_base = 1000000.0


def partner_2(value, axis, bit):
    mask = 2**bit
    pairs = [(source, source ^ mask) for source in range(lax.axis_size(axis))]
    return lax.ppermute(value, axis, pairs)


def row_norm(inputs, gain):
    inputs = inputs.astype(jnp.float32)
    scale = lax.rsqrt(jnp.mean(inputs * inputs, axis=-1, keepdims=True) + epsilon)
    return inputs * scale * gain.astype(jnp.float32)


def rotate(inputs, position):
    half_dim = inputs.shape[-1] // 2
    frequency = rope_base ** (-2.0 * jnp.arange(half_dim, dtype=jnp.float32) / inputs.shape[-1])
    angles = position.astype(jnp.float32)[:, None] * frequency[None, :]
    cosine = jnp.cos(angles)[:, None, :]
    sine_part = jnp.sin(angles)[:, None, :]
    front = inputs[..., :half_dim]
    second = inputs[..., half_dim:]
    return jnp.concatenate(
        [front * cosine - second * sine_part, second * cosine + front * sine_part], axis=-1
    )


def prompt_layout(lengths_row, token_count):
    prompt_ends = jnp.cumsum(lengths_row)
    prompt_starts = prompt_ends - lengths_row
    row_ids = jnp.arange(token_count, dtype=jnp.int32)
    prompt = jnp.sum((row_ids[:, None] >= prompt_ends[None, :]).astype(jnp.int32), axis=1)
    inside = (row_ids[:, None] >= prompt_starts[None, :]) & (
        row_ids[:, None] < prompt_ends[None, :]
    )
    offset = jnp.sum(jnp.where(inside, prompt_starts[None, :], 0), axis=1)
    return (prompt, row_ids - offset, prompt_starts, prompt_ends)


def per_device(
    stream,
    lengths,
    page_table,
    request_prompt,
    attn_gain,
    query_gain,
    key_gain,
    mlp_gain,
    w_query,
    key_value_weight,
    w_out,
    w_gate,
    w_up,
    w_down,
):
    tok_dev = stream.shape[0]
    tensor_element_count = lax.axis_size("tensor")
    token_count = tok_dev * tensor_element_count
    my_index = lax.axis_index("tensor")
    heads_dev = w_query.shape[1] // HEAD_SIZE
    query_cols = heads_dev * HEAD_SIZE
    prompt, position, prompt_starts, prompt_ends = prompt_layout(lengths[0], token_count)
    portion = lax.all_gather(
        row_norm(stream, attn_gain).astype(jnp.bfloat16), "tensor", axis=0, tiled=True
    )
    joined = jnp.concatenate(
        [
            jnp.dot(portion, w_query, preferred_element_type=jnp.float32),
            jnp.dot(portion, key_value_weight, preferred_element_type=jnp.float32),
        ],
        axis=1,
    )
    queries = joined[:, :query_cols].reshape(token_count, heads_dev, HEAD_SIZE)
    kv_part = joined[:, query_cols:].astype(jnp.bfloat16)
    key_value_group = tensor_element_count // KEY_VALUE_HEADS
    for bit_id in range(key_value_group.bit_length() - 1):
        partner = partner_2(kv_part, "tensor", bit_id)
        upper_half = my_index // 2**bit_id % 2
        kv_part = jnp.where(
            upper_half == 1,
            jnp.concatenate([partner, kv_part], axis=1),
            jnp.concatenate([kv_part, partner], axis=1),
        )
    key_flat = rotate(row_norm(kv_part[:, None, :HEAD_SIZE], key_gain), position).astype(
        jnp.bfloat16
    )[:, 0, :]
    value_matrix_rows = kv_part[:, HEAD_SIZE:]
    q_rot = rotate(row_norm(queries, query_gain), position).astype(jnp.bfloat16)
    piece_cols = key_value_weight.shape[1]
    head_rows = jnp.concatenate([key_flat, value_matrix_rows], axis=1)
    own_cols = lax.dynamic_slice_in_dim(
        head_rows, my_index % key_value_group * piece_cols, piece_cols, 1
    )
    page_count = token_count // PAGE_TOKENS
    page_rows = own_cols.reshape(page_count, PAGE_TOKENS, piece_cols)
    group_count = lax.axis_size("dp")
    capacity = page_count // group_count
    owners = page_table // page_count
    slot_ids = page_table % page_count
    hits = (owners[:, None] == jnp.arange(group_count, dtype=jnp.int32)[None, :]).astype(jnp.int32)
    order_in = jnp.sum((jnp.cumsum(hits, axis=0) - hits) * hits, axis=1)
    buffer_pos = owners * capacity + order_in
    source = (
        jnp.zeros((page_count,), jnp.int32)
        .at[buffer_pos]
        .set(jnp.arange(page_count, dtype=jnp.int32))
    )
    send_pages = page_rows[source].reshape(group_count, capacity, PAGE_TOKENS, piece_cols)
    send_slots = slot_ids[source].reshape(group_count, capacity)
    got_pages, got_slots = (
        lax.all_to_all(send_pages, "dp", split_axis=0, concat_axis=0, tiled=True),
        lax.all_to_all(send_slots, "dp", split_axis=0, concat_axis=0, tiled=True),
    )
    paged_key_value_cache = (
        jnp.zeros((page_count, PAGE_TOKENS, piece_cols), jnp.bfloat16)
        .at[got_slots.reshape(-1)]
        .set(got_pages.reshape(page_count, PAGE_TOKENS, piece_cols))
    )
    block_rows = min(512, token_count)
    block_total = token_count // block_rows
    score_scale = math.sqrt(HEAD_SIZE)
    all_ids = jnp.arange(token_count, dtype=jnp.int32)
    local_ids = jnp.arange(block_rows, dtype=jnp.int32)

    def dense_block(block_index):
        first_row = block_index * block_rows
        q_block = lax.dynamic_slice_in_dim(q_rot, first_row, block_rows, 0)
        q_prompt = lax.dynamic_slice_in_dim(prompt, first_row, block_rows, 0)
        row_ids = first_row + local_ids
        scores = (
            jnp.einsum("qhd,kd->hqk", q_block, key_flat, preferred_element_type=jnp.float32)
            / score_scale
        )
        allowed = ((q_prompt[:, None] == prompt[None, :]) & (row_ids[:, None] >= all_ids[None, :]))[
            None
        ]
        peak = jnp.max(jnp.where(allowed, scores, -jnp.inf), axis=2, keepdims=True)
        weight = jnp.where(allowed, jnp.exp(scores - peak), 0.0)
        total_weight = jnp.sum(weight, axis=2, keepdims=True)
        running = jnp.einsum(
            "hqk,kd->hqd",
            weight.astype(jnp.bfloat16),
            value_matrix_rows,
            preferred_element_type=jnp.float32,
        )
        return (running / total_weight).astype(jnp.bfloat16)

    block_ids = jnp.arange(block_total, dtype=jnp.int32)
    blocks_out = lax.map(dense_block, block_ids)
    attn = jnp.transpose(blocks_out, (0, 2, 1, 3)).reshape(token_count, query_cols)
    attn_sum = lax.psum_scatter(
        jnp.dot(attn, w_out, preferred_element_type=jnp.float32).astype(jnp.bfloat16),
        "tensor",
        scatter_dimension=0,
        tiled=True,
    ).astype(jnp.float32)
    resid = (stream.astype(jnp.float32) + attn_sum).astype(jnp.bfloat16)
    portion = lax.all_gather(
        row_norm(resid, mlp_gain).astype(jnp.bfloat16), "tensor", axis=0, tiled=True
    )
    gate_rows = jnp.dot(portion, w_gate, preferred_element_type=jnp.float32)
    upward = jnp.dot(portion, w_up, preferred_element_type=jnp.float32)
    hidden = (jax.nn.silu(gate_rows) * upward).astype(jnp.bfloat16)
    mlp_sum = lax.psum_scatter(
        jnp.dot(hidden, w_down, preferred_element_type=jnp.float32).astype(jnp.bfloat16),
        "tensor",
        scatter_dimension=0,
        tiled=True,
    ).astype(jnp.float32)
    layer_out = (resid.astype(jnp.float32) + mlp_sum).astype(jnp.bfloat16)
    my_rows = my_index * tok_dev + jnp.arange(tok_dev, dtype=jnp.int32)
    select = ((prompt_ends - 1)[:, None] == my_rows[None, :]).astype(jnp.bfloat16)
    end_terms = jnp.dot(select, layer_out, preferred_element_type=jnp.float32)
    end_rows = lax.psum_scatter(
        end_terms.astype(jnp.bfloat16), "tensor", scatter_dimension=1, tiled=True
    )
    table = lax.all_gather(end_rows, "dp", axis=0, tiled=True)
    pick = (request_prompt[:, None] == jnp.arange(table.shape[0], dtype=jnp.int32)[None, :]).astype(
        jnp.bfloat16
    )
    request_state = jnp.dot(pick, table, preferred_element_type=jnp.float32).astype(jnp.bfloat16)
    return (layer_out, paged_key_value_cache, request_state)


def fused_kernel(
    lengths_ref,
    page_ref,
    request_ref,
    stream_ref,
    attn_gain_ref,
    query_gain_ref,
    key_gain_ref,
    mlp_gain_ref,
    frequency_ref,
    wq_hbm,
    wkv_hbm,
    wo_hbm,
    wg_hbm,
    wu_hbm,
    wd_hbm,
    layer_ref,
    cache_ref,
    state_ref,
    wq,
    wkv,
    wo,
    wg,
    wu,
    wd,
    gathered,
    q_rot,
    kv_all,
    slots_all,
    attn,
    hidden,
    part,
    y_in,
    z_out,
    z_in,
    cosine,
    sine,
    starts,
    resid,
    end_out,
    end_in,
    table,
    weight_sem,
    ag_recv,
    ag_zsend,
    ag_ysend,
    rs_yrecv,
    rs_ysend,
    rs_zrecv,
    rs_zsend,
    kv_send,
    kv_recv,
    slots_send,
    slots_recv,
    end_send,
    end_recv,
    table_send,
    table_recv,
):
    f32 = jnp.float32
    bf16 = jnp.bfloat16
    t = lax.axis_index("tensor")
    g = lax.axis_index("dp")
    z = t // 2
    y = t % 2
    rows = stream_ref.shape[0]
    width = stream_ref.shape[1]
    tokens = rows * 8

    pairs = ((wq_hbm, wq), (wkv_hbm, wkv), (wo_hbm, wo), (wg_hbm, wg), (wu_hbm, wu), (wd_hbm, wd))
    loads = [
        pltpu.make_async_copy(source, target, weight_sem.at[k])
        for k, (source, target) in enumerate(pairs)
    ]
    for load in loads:
        load.start()

    barrier = pltpu.get_barrier_semaphore()
    for k in range(1, 8):
        pl.semaphore_signal(barrier, inc=1, device_id=(g, (t + k) % 8), device_id_type=MESH)
    for k in range(1, 4):
        pl.semaphore_signal(barrier, inc=1, device_id=((g + k) % 4, t), device_id_type=MESH)

    def normed(value, gain_ref):
        scale = lax.rsqrt(jnp.mean(value * value, axis=-1, keepdims=True) + epsilon)
        return value * scale * gain_ref[...].astype(f32)

    gathered[0, t] = normed(stream_ref[...].astype(f32), attn_gain_ref).astype(bf16)
    pl.semaphore_wait(barrier, 10)

    def y_copy(source, target, send, recv):
        return pltpu.make_async_remote_copy(
            src_ref=source, dst_ref=target, send_sem=send, recv_sem=recv,
            device_id=(g, z * 2 + 1 - y), device_id_type=MESH)

    def z_copy(source, target, send, recv, step):
        return pltpu.make_async_remote_copy(
            src_ref=source, dst_ref=target, send_sem=send, recv_sem=recv,
            device_id=(g, (z + step) * 2 + y), device_id_type=MESH)

    def gather(phase, before, process, after):
        def up(s):
            slot = (z - s) * 2 + y
            return z_copy(gathered.at[phase, slot], gathered.at[phase, slot],
                          ag_zsend.at[phase, 0, s], ag_recv.at[phase, slot], 1)

        def down(s):
            slot = (z + s) * 2 + y
            return z_copy(gathered.at[phase, slot], gathered.at[phase, slot],
                          ag_zsend.at[phase, 1, s], ag_recv.at[phase, slot], -1)

        def across(level):
            slot = level * 2 + y
            return y_copy(gathered.at[phase, slot], gathered.at[phase, slot],
                          ag_ysend.at[phase, level], ag_recv.at[phase, slot])

        def arrived(slot):
            y_copy(gathered.at[phase, slot], gathered.at[phase, slot],
                   ag_ysend.at[phase, 0], ag_recv.at[phase, slot]).wait_recv()

        def group(level):
            arrived(level * 2 + 1 - y)
            process(level)

        def groups(s):
            if s == 0:
                group(z)
            else:
                pl.when(z - s >= 0)(lambda: group(z - s))
                pl.when(z + s <= 3)(lambda: group(z + s))

        for s in range(4):
            if s:
                @pl.when(z - s >= 0)
                def _():
                    arrived((z - s) * 2 + y)

                    @pl.when(z < 3)
                    def _():
                        up(s).start()

                    across(z - s).start()

                @pl.when(z + s <= 3)
                def _():
                    arrived((z + s) * 2 + y)

                    @pl.when(z > 0)
                    def _():
                        down(s).start()

                    across(z + s).start()

                groups(s - 1)
                if s == 3:
                    after()
            else:
                pl.when(z < 3)(lambda: up(0).start())
                pl.when(z > 0)(lambda: down(0).start())
                across(z).start()
                before()
        groups(3)

        for s in range(4):
            pl.when((z - s >= 0) & (z < 3))(lambda: up(s).wait_send())
            pl.when((z + s <= 3) & (z > 0))(lambda: down(s).wait_send())
            across(s).wait_send()

    packed = 27 + 72 * z - 15 * (z * (z - 1) // 2) + 5 * (z * (z - 1) * (z - 2))
    order = [packed % 4, packed // 4 % 4, packed // 16 % 4, packed // 64]

    piece = 512
    pieces = width // piece

    def columns(p):
        return pl.ds(pl.multiple_of(p * piece, piece), piece)

    def send_part(phase, level, p):
        return y_copy(part.at[phase, level, 1 - y, :, columns(p)],
                      y_in.at[phase, level, :, columns(p)],
                      rs_ysend.at[phase, level, p], rs_yrecv.at[phase, level, p])

    def flow(phase, level, direction, step, p):
        return z_copy(z_out.at[phase, level, :, columns(p)],
                      z_in.at[phase, direction, level, :, columns(p)],
                      rs_zsend.at[phase, level, p], rs_zrecv.at[phase, direction, level, p], step)

    def forward(phase, level, p):
        cols = columns(p)
        send_part(phase, level, p).wait_recv()
        z_out[phase, level, :, cols] = (
            part[phase, level, y, :, cols].astype(f32) + y_in[phase, level, :, cols].astype(f32)
        ).astype(bf16)

        def onward(direction, step, inner):
            @pl.when(inner)
            def _():
                flow(phase, level, direction, step, p).wait_recv()
                z_out[phase, level, :, cols] = (
                    part[phase, level, y, :, cols].astype(f32)
                    + y_in[phase, level, :, cols].astype(f32)
                    + z_in[phase, direction, level, :, cols].astype(f32)
                ).astype(bf16)

            flow(phase, level, direction, step, p).start()

        pl.when(level > z)(lambda: onward(0, 1, z > 0))
        pl.when(level < z)(lambda: onward(1, -1, z < 3))

    def collect(phase):
        @pl.loop(0, pieces)
        def _(p):
            cols = columns(p)
            send_part(phase, z, p).wait_recv()
            resid[1, :, cols] = (
                part[phase, z, y, :, cols].astype(f32) + y_in[phase, z, :, cols].astype(f32))

            @pl.when(z > 0)
            def _():
                flow(phase, z, 0, 1, p).wait_recv()
                resid[1, :, cols] = resid[1, :, cols] + z_in[phase, 0, z, :, cols].astype(f32)

            @pl.when(z < 3)
            def _():
                flow(phase, z, 1, -1, p).wait_recv()
                resid[1, :, cols] = resid[1, :, cols] + z_in[phase, 1, z, :, cols].astype(f32)

    def sent(phase):
        @pl.loop(0, pieces)
        def _(p):
            for level in range(4):
                send_part(phase, level, p).wait_send()
                pl.when(z != level)(lambda: flow(phase, level, 0, 1, p).wait_send())

    def angles():
        ids = lax.broadcasted_iota(jnp.int32, (tokens, HEAD_SIZE), 0)
        begin = jnp.int32(0)
        offset = jnp.zeros((tokens, HEAD_SIZE), jnp.int32)
        for k in range(lengths_ref.shape[1]):
            end = begin + lengths_ref[0, k]
            offset = jnp.where((ids >= begin) & (ids < end), begin, offset)
            begin = end
        starts[...] = offset
        angle = (ids - offset).astype(f32) * frequency_ref[...]
        lane = lax.broadcasted_iota(jnp.int32, (tokens, HEAD_SIZE), 1)
        cosine[...] = jnp.cos(angle)
        signed = jnp.sin(angle)
        sine[...] = jnp.where(lane < HEAD_SIZE // 2, -signed, signed)
        token = lax.broadcasted_iota(jnp.int32, slots_all.shape[1:], 1)
        slots = jnp.zeros(slots_all.shape[1:], jnp.int32)
        for k in range(page_ref.shape[0]):
            slots = jnp.where(token // PAGE_TOKENS == k, page_ref[k], slots)
        slots_all[0] = slots * PAGE_TOKENS + token % PAGE_TOKENS
        loads[0].wait()
        loads[1].wait()

    heads = wq.shape[1] // HEAD_SIZE

    def project(level):
        inputs = gathered[0, pl.ds(level * 2, 2)].reshape(2 * rows, width)
        span = pl.ds(pl.multiple_of(level * 2 * rows, 32), 2 * rows)
        cos_rows = cosine[span, :]
        sin_rows = sine[span, :]

        def rotated(value):
            return value * cos_rows + pltpu.roll(value, HEAD_SIZE // 2, 1) * sin_rows

        for pair in range(heads // 2):
            block = jnp.dot(inputs, wq[:, pair * 256:(pair + 1) * 256], preferred_element_type=f32)
            for k in range(2):
                head = block[:, k * HEAD_SIZE:(k + 1) * HEAD_SIZE]
                q_rot[pair * 2 + k, span, :] = rotated(normed(head, query_gain_ref)).astype(bf16)
        keyval = jnp.dot(inputs, wkv[...], preferred_element_type=f32).astype(bf16)
        key_head = keyval[:, :HEAD_SIZE].astype(f32)
        kv_all[0, span, :HEAD_SIZE] = rotated(normed(key_head, key_gain_ref)).astype(bf16)
        kv_all[0, span, HEAD_SIZE:] = keyval[:, HEAD_SIZE:]

    gather(0, angles, project, lambda: None)

    def kv_copies(k):
        peer = (lax.rem(g + k, 4), t)
        return (
            pltpu.make_async_remote_copy(
                src_ref=kv_all.at[0], dst_ref=kv_all.at[k], send_sem=kv_send.at[k],
                recv_sem=kv_recv.at[k], device_id=peer, device_id_type=MESH),
            pltpu.make_async_remote_copy(
                src_ref=slots_all.at[0], dst_ref=slots_all.at[k], send_sem=slots_send.at[k],
                recv_sem=slots_recv.at[k], device_id=peer, device_id_type=MESH),
        )

    for k in range(1, 4):
        for copy in kv_copies(k):
            copy.start()

    tile = 256
    group_rows = 2 * rows
    loads[2].wait()
    for i in range(4):
        level = order[i]
        first_row = pl.multiple_of(level * group_rows, 32)
        span = pl.ds(first_row, group_rows)
        row_id = first_row + lax.broadcasted_iota(jnp.int32, (group_rows, tokens), 0)
        key_id = lax.broadcasted_iota(jnp.int32, (group_rows, tokens), 1)
        begin = jnp.concatenate([starts[span, :]] * (tokens // HEAD_SIZE), axis=1)
        allowed = (key_id >= begin) & (key_id <= row_id)
        for head in range(heads):
            scores = lax.dot_general(
                q_rot[head, span, :], kv_all[0, :, :HEAD_SIZE], (((1,), (1,)), ((), ())),
                preferred_element_type=f32) * (1.0 / math.sqrt(HEAD_SIZE))
            scores = jnp.where(allowed, scores, -jnp.inf)
            peak = jnp.max(scores, axis=1, keepdims=True)
            weight = jnp.exp(scores - peak)
            total_weight = jnp.sum(weight, axis=1, keepdims=True)
            mixed = jnp.dot(
                weight.astype(bf16), kv_all[0, :, HEAD_SIZE:], preferred_element_type=f32)
            attn[:, head * HEAD_SIZE:(head + 1) * HEAD_SIZE] = (mixed / total_weight).astype(bf16)
        inputs = attn[...]

        @pl.loop(0, pieces)
        def _(p):
            cols = columns(p)
            out = jnp.dot(inputs, wo[:, cols], preferred_element_type=f32)
            part[0, level, :, :, cols] = out.astype(bf16).reshape(2, rows, piece)
            send_part(0, level, p).start()

    for i in range(3):

        @pl.loop(0, pieces)
        def _(p):
            forward(0, order[i], p)

    collect(0)
    residual = (stream_ref[...].astype(f32) + resid[1]).astype(bf16)
    resid[0] = residual.astype(f32)
    gathered[1, t] = normed(resid[0], mlp_gain_ref).astype(bf16)

    def fill_cache():
        row = g * tokens + lax.broadcasted_iota(jnp.int32, (tokens, tokens), 0)
        total = None
        for k in range(4):
            if k:
                for copy in kv_copies(k):
                    copy.wait()
            pick = (slots_all[k, 0:1, :] == row).astype(f32).astype(bf16)
            term = jnp.dot(pick, kv_all[k], preferred_element_type=f32)
            total = term if total is None else total + term
        cache_ref[...] = total.astype(bf16)
        loads[3].wait()
        loads[4].wait()
        loads[5].wait()

    hidden_width = wg.shape[0]

    across_cols = (((1,), (1,)), ((), ()))

    def feed_forward(level):
        inputs = gathered[1, pl.ds(level * 2, 2)].reshape(2 * rows, width)
        for start in range(0, hidden_width, tile):
            stop = min(start + tile, hidden_width)
            gate = lax.dot_general(inputs, wg[start:stop, :], across_cols, preferred_element_type=f32)
            upward = lax.dot_general(inputs, wu[start:stop, :], across_cols, preferred_element_type=f32)
            hidden[:, start:stop] = (gate / (1.0 + jnp.exp(-gate)) * upward).astype(bf16)
        inner = hidden[...]

        @pl.loop(0, pieces)
        def _(p):
            cols = columns(p)
            out = jnp.dot(inner, wd[:, cols], preferred_element_type=f32)
            part[1, level, :, :, cols] = out.astype(bf16).reshape(2, rows, piece)
            send_part(1, level, p).start()

    outer = (z == 0) | (z == 3)

    def early():
        @pl.when(outer)
        def _():
            @pl.loop(0, pieces)
            def _(p):
                forward(1, order[2], p)

    gather(1, fill_cache, feed_forward, early)

    @pl.when(outer)
    def _():
        for i in (1, 0):

            @pl.loop(0, pieces)
            def _(p):
                forward(1, order[i], p)

    @pl.when(jnp.logical_not(outer))
    def _():
        @pl.loop(0, pieces)
        def _(p):
            forward(1, order[2], p)

        @pl.loop(0, pieces)
        def _(p):
            forward(1, order[0], p)
            forward(1, order[1], p)

    collect(1)
    layer_out = (resid[0] + resid[1]).astype(bf16)
    layer_ref[...] = layer_out

    slots = end_out.shape[1]
    span_cols = end_out.shape[2]
    row_id = t * rows + lax.broadcasted_iota(jnp.int32, (slots, rows), 1)
    slot_id = lax.broadcasted_iota(jnp.int32, (slots, rows), 0)
    end = jnp.int32(0)
    hit = jnp.zeros((slots, rows), f32)
    for k in range(lengths_ref.shape[1]):
        end = end + lengths_ref[0, k]
        hit = jnp.where((slot_id == k) & (row_id == end - 1), 1.0, hit)
    terms = jnp.dot(hit.astype(bf16), layer_out, preferred_element_type=f32).astype(bf16)
    for k in range(8):
        first = k * 5 // 2 * 128
        end_out[k] = terms[:, first:first + span_cols]

    def end_copy(k):
        peer = lax.rem(t + k, 8)
        return pltpu.make_async_remote_copy(
            src_ref=end_out.at[peer], dst_ref=end_in.at[k], send_sem=end_send.at[k],
            recv_sem=end_recv.at[k], device_id=(g, peer), device_id_type=MESH)

    for k in range(1, 8):
        end_copy(k).start()
    total = end_out[t].astype(f32)
    for k in range(1, 8):
        end_copy(k).wait()
        total = total + end_in[k].astype(f32)
    table[0] = total.astype(bf16)

    def table_copy(k):
        return pltpu.make_async_remote_copy(
            src_ref=table.at[0], dst_ref=table.at[k], send_sem=table_send.at[k],
            recv_sem=table_recv.at[k], device_id=(lax.rem(g + k, 4), t), device_id_type=MESH)

    for k in range(1, 4):
        table_copy(k).start()
    prompts = lengths_ref.shape[1]
    requests = request_ref.shape[0]
    line = lax.broadcasted_iota(jnp.int32, (requests, slots), 0)
    column = lax.broadcasted_iota(jnp.int32, (requests, slots), 1)
    asked = jnp.zeros((requests, slots), jnp.int32)
    for k in range(requests):
        asked = jnp.where(line == k, request_ref[k], asked)
    state = None
    for k in range(4):
        if k:
            table_copy(k).wait()
        batch = lax.rem(g + 4 - k, 4)
        pick = ((asked == batch * prompts + column) & (column < prompts)).astype(f32).astype(bf16)
        term = jnp.dot(pick, table[k], preferred_element_type=f32)
        state = term if state is None else state + term
    sent(0)
    sent(1)
    keep = state_ref.shape[1]
    shifted = state[:, span_cols - keep:]
    state_ref[...] = jnp.where(t % 2 == 1, shifted, state[:, :keep]).astype(bf16)


def fused_device(
    stream,
    lengths,
    page_table,
    request_prompt,
    attn_gain,
    query_gain,
    key_gain,
    mlp_gain,
    w_query,
    key_value_weight,
    w_out,
    w_gate,
    w_up,
    w_down,
):
    rows, width = stream.shape
    tokens = rows * 8
    query_cols = w_query.shape[1]
    keyval_cols = key_value_weight.shape[1]
    hidden_width = w_gate.shape[1]
    heads = query_cols // HEAD_SIZE
    requests = request_prompt.shape[0]
    state_cols = width // 8
    pieces = width // 512
    exponents = -2.0 * (np.arange(HEAD_SIZE) % (HEAD_SIZE // 2)) / HEAD_SIZE
    frequency = np.power(rope_base, exponents).astype(np.float32)[None, :]
    bf16 = jnp.bfloat16
    f32 = jnp.float32
    vmem = pl.BlockSpec(memory_space=pltpu.VMEM)
    smem = pl.BlockSpec(memory_space=pltpu.SMEM)
    hbm = pl.BlockSpec(memory_space=pl.ANY)
    dma = pltpu.SemaphoreType.DMA
    layer_out, cache, state = pl.pallas_call(
        fused_kernel,
        out_shape=(
            jax.ShapeDtypeStruct((rows, width), bf16),
            jax.ShapeDtypeStruct((tokens, keyval_cols), bf16),
            jax.ShapeDtypeStruct((requests, state_cols), bf16),
        ),
        in_specs=[smem] * 3 + [vmem] * 6 + [hbm] * 6,
        out_specs=(vmem, vmem, vmem),
        scratch_shapes=[
            pltpu.VMEM((width, query_cols), bf16),
            pltpu.VMEM((width, keyval_cols), bf16),
            pltpu.VMEM((query_cols, width), bf16),
            pltpu.VMEM((hidden_width, width), bf16),
            pltpu.VMEM((hidden_width, width), bf16),
            pltpu.VMEM((hidden_width, width), bf16),
            pltpu.VMEM((2, 8, rows, width), bf16),
            pltpu.VMEM((heads, tokens, HEAD_SIZE), bf16),
            pltpu.VMEM((4, tokens, keyval_cols), bf16),
            pltpu.VMEM((4, 8, tokens), jnp.int32),
            pltpu.VMEM((2 * rows, query_cols), bf16),
            pltpu.VMEM((2 * rows, hidden_width), bf16),
            pltpu.VMEM((2, 4, 2, rows, width), bf16),
            pltpu.VMEM((2, 4, rows, width), bf16),
            pltpu.VMEM((2, 4, rows, width), bf16),
            pltpu.VMEM((2, 2, 4, rows, width), bf16),
            pltpu.VMEM((tokens, HEAD_SIZE), f32),
            pltpu.VMEM((tokens, HEAD_SIZE), f32),
            pltpu.VMEM((tokens, HEAD_SIZE), jnp.int32),
            pltpu.VMEM((2, rows, width), f32),
            pltpu.VMEM((8, 16, 384), bf16),
            pltpu.VMEM((8, 16, 384), bf16),
            pltpu.VMEM((4, 16, 384), bf16),
            dma((6,)),
            dma((2, 8)),
            dma((2, 2, 4)),
            dma((2, 4)),
            dma((2, 4, pieces)),
            dma((2, 4, pieces)),
            dma((2, 2, 4, pieces)),
            dma((2, 4, pieces)),
            dma((4,)),
            dma((4,)),
            dma((4,)),
            dma((4,)),
            dma((8,)),
            dma((8,)),
            dma((4,)),
            dma((4,)),
        ],
        compiler_params=pltpu.CompilerParams(
            collective_id=0, has_side_effects=True, vmem_limit_bytes=60 * 1024 * 1024
        ),
        name="fused_layer",
    )(
        lengths, page_table, request_prompt, stream, attn_gain[None, :], query_gain[None, :], key_gain[None, :],
        mlp_gain[None, :], frequency, w_query, key_value_weight, w_out, w_gate.T, w_up.T, w_down,
    )
    return layer_out, cache.reshape(tokens // PAGE_TOKENS, PAGE_TOKENS, keyval_cols), state


def solution(mesh):
    placed = (
        P(("dp", "tensor"), None),
        P("dp", None),
        P("dp"),
        P("dp"),
        P(),
        P(),
        P(),
        P(),
        P(None, "tensor"),
        P(None, "tensor"),
        P("tensor", None),
        P(None, "tensor"),
        P(None, "tensor"),
        P("tensor", None),
    )
    fused = mesh.shape["tensor"] == KEY_VALUE_HEADS and mesh.shape["dp"] == 4
    return jax.shard_map(
        fused_device if fused else per_device,
        mesh=mesh,
        in_specs=placed,
        out_specs=(P(("dp", "tensor"), None), P("dp", None, "tensor"), P("dp", "tensor")),
        check_vma=False,
    )
```

```python
import math

import jax
import jax.numpy as jnp
import numpy as np
from jax import lax
from jax.experimental import pallas as pl
from jax.experimental.pallas import tpu as pltpu
from jax.sharding import PartitionSpec as P

KEY_VALUE_HEADS = 8
HEAD_SIZE = 128
PAGE_TOKENS = 16
MESH = pl.DeviceIdType.MESH


epsilon = 1e-06
rope_base = 1000000.0


def partner_2(value, axis, bit):
    mask = 2**bit
    pairs = [(source, source ^ mask) for source in range(lax.axis_size(axis))]
    return lax.ppermute(value, axis, pairs)


def row_norm(inputs, gain):
    inputs = inputs.astype(jnp.float32)
    scale = lax.rsqrt(jnp.mean(inputs * inputs, axis=-1, keepdims=True) + epsilon)
    return inputs * scale * gain.astype(jnp.float32)


def rotate(inputs, position):
    half_dim = inputs.shape[-1] // 2
    frequency = rope_base ** (-2.0 * jnp.arange(half_dim, dtype=jnp.float32) / inputs.shape[-1])
    angles = position.astype(jnp.float32)[:, None] * frequency[None, :]
    cosine = jnp.cos(angles)[:, None, :]
    sine_part = jnp.sin(angles)[:, None, :]
    front = inputs[..., :half_dim]
    second = inputs[..., half_dim:]
    return jnp.concatenate(
        [front * cosine - second * sine_part, second * cosine + front * sine_part], axis=-1
    )


def prompt_layout(lengths_row, token_count):
    prompt_ends = jnp.cumsum(lengths_row)
    prompt_starts = prompt_ends - lengths_row
    row_ids = jnp.arange(token_count, dtype=jnp.int32)
    prompt = jnp.sum((row_ids[:, None] >= prompt_ends[None, :]).astype(jnp.int32), axis=1)
    inside = (row_ids[:, None] >= prompt_starts[None, :]) & (
        row_ids[:, None] < prompt_ends[None, :]
    )
    offset = jnp.sum(jnp.where(inside, prompt_starts[None, :], 0), axis=1)
    return (prompt, row_ids - offset, prompt_starts, prompt_ends)


def per_device(
    stream,
    lengths,
    page_table,
    request_prompt,
    attn_gain,
    query_gain,
    key_gain,
    mlp_gain,
    w_query,
    key_value_weight,
    w_out,
    w_gate,
    w_up,
    w_down,
):
    tok_dev = stream.shape[0]
    tensor_element_count = lax.axis_size("tensor")
    token_count = tok_dev * tensor_element_count
    my_index = lax.axis_index("tensor")
    heads_dev = w_query.shape[1] // HEAD_SIZE
    query_cols = heads_dev * HEAD_SIZE
    prompt, position, prompt_starts, prompt_ends = prompt_layout(lengths[0], token_count)
    portion = lax.all_gather(
        row_norm(stream, attn_gain).astype(jnp.bfloat16), "tensor", axis=0, tiled=True
    )
    joined = jnp.concatenate(
        [
            jnp.dot(portion, w_query, preferred_element_type=jnp.float32),
            jnp.dot(portion, key_value_weight, preferred_element_type=jnp.float32),
        ],
        axis=1,
    )
    queries = joined[:, :query_cols].reshape(token_count, heads_dev, HEAD_SIZE)
    kv_part = joined[:, query_cols:].astype(jnp.bfloat16)
    key_value_group = tensor_element_count // KEY_VALUE_HEADS
    for bit_id in range(key_value_group.bit_length() - 1):
        partner = partner_2(kv_part, "tensor", bit_id)
        upper_half = my_index // 2**bit_id % 2
        kv_part = jnp.where(
            upper_half == 1,
            jnp.concatenate([partner, kv_part], axis=1),
            jnp.concatenate([kv_part, partner], axis=1),
        )
    key_flat = rotate(row_norm(kv_part[:, None, :HEAD_SIZE], key_gain), position).astype(
        jnp.bfloat16
    )[:, 0, :]
    value_matrix_rows = kv_part[:, HEAD_SIZE:]
    q_rot = rotate(row_norm(queries, query_gain), position).astype(jnp.bfloat16)
    piece_cols = key_value_weight.shape[1]
    head_rows = jnp.concatenate([key_flat, value_matrix_rows], axis=1)
    own_cols = lax.dynamic_slice_in_dim(
        head_rows, my_index % key_value_group * piece_cols, piece_cols, 1
    )
    page_count = token_count // PAGE_TOKENS
    page_rows = own_cols.reshape(page_count, PAGE_TOKENS, piece_cols)
    group_count = lax.axis_size("dp")
    capacity = page_count // group_count
    owners = page_table // page_count
    slot_ids = page_table % page_count
    hits = (owners[:, None] == jnp.arange(group_count, dtype=jnp.int32)[None, :]).astype(jnp.int32)
    order_in = jnp.sum((jnp.cumsum(hits, axis=0) - hits) * hits, axis=1)
    buffer_pos = owners * capacity + order_in
    source = (
        jnp.zeros((page_count,), jnp.int32)
        .at[buffer_pos]
        .set(jnp.arange(page_count, dtype=jnp.int32))
    )
    send_pages = page_rows[source].reshape(group_count, capacity, PAGE_TOKENS, piece_cols)
    send_slots = slot_ids[source].reshape(group_count, capacity)
    got_pages, got_slots = (
        lax.all_to_all(send_pages, "dp", split_axis=0, concat_axis=0, tiled=True),
        lax.all_to_all(send_slots, "dp", split_axis=0, concat_axis=0, tiled=True),
    )
    paged_key_value_cache = (
        jnp.zeros((page_count, PAGE_TOKENS, piece_cols), jnp.bfloat16)
        .at[got_slots.reshape(-1)]
        .set(got_pages.reshape(page_count, PAGE_TOKENS, piece_cols))
    )
    block_rows = min(512, token_count)
    block_total = token_count // block_rows
    score_scale = math.sqrt(HEAD_SIZE)
    all_ids = jnp.arange(token_count, dtype=jnp.int32)
    local_ids = jnp.arange(block_rows, dtype=jnp.int32)

    def dense_block(block_index):
        first_row = block_index * block_rows
        q_block = lax.dynamic_slice_in_dim(q_rot, first_row, block_rows, 0)
        q_prompt = lax.dynamic_slice_in_dim(prompt, first_row, block_rows, 0)
        row_ids = first_row + local_ids
        scores = (
            jnp.einsum("qhd,kd->hqk", q_block, key_flat, preferred_element_type=jnp.float32)
            / score_scale
        )
        allowed = ((q_prompt[:, None] == prompt[None, :]) & (row_ids[:, None] >= all_ids[None, :]))[
            None
        ]
        peak = jnp.max(jnp.where(allowed, scores, -jnp.inf), axis=2, keepdims=True)
        weight = jnp.where(allowed, jnp.exp(scores - peak), 0.0)
        total_weight = jnp.sum(weight, axis=2, keepdims=True)
        running = jnp.einsum(
            "hqk,kd->hqd",
            weight.astype(jnp.bfloat16),
            value_matrix_rows,
            preferred_element_type=jnp.float32,
        )
        return (running / total_weight).astype(jnp.bfloat16)

    block_ids = jnp.arange(block_total, dtype=jnp.int32)
    blocks_out = lax.map(dense_block, block_ids)
    attn = jnp.transpose(blocks_out, (0, 2, 1, 3)).reshape(token_count, query_cols)
    attn_sum = lax.psum_scatter(
        jnp.dot(attn, w_out, preferred_element_type=jnp.float32).astype(jnp.bfloat16),
        "tensor",
        scatter_dimension=0,
        tiled=True,
    ).astype(jnp.float32)
    resid = (stream.astype(jnp.float32) + attn_sum).astype(jnp.bfloat16)
    portion = lax.all_gather(
        row_norm(resid, mlp_gain).astype(jnp.bfloat16), "tensor", axis=0, tiled=True
    )
    gate_rows = jnp.dot(portion, w_gate, preferred_element_type=jnp.float32)
    upward = jnp.dot(portion, w_up, preferred_element_type=jnp.float32)
    hidden = (jax.nn.silu(gate_rows) * upward).astype(jnp.bfloat16)
    mlp_sum = lax.psum_scatter(
        jnp.dot(hidden, w_down, preferred_element_type=jnp.float32).astype(jnp.bfloat16),
        "tensor",
        scatter_dimension=0,
        tiled=True,
    ).astype(jnp.float32)
    layer_out = (resid.astype(jnp.float32) + mlp_sum).astype(jnp.bfloat16)
    my_rows = my_index * tok_dev + jnp.arange(tok_dev, dtype=jnp.int32)
    select = ((prompt_ends - 1)[:, None] == my_rows[None, :]).astype(jnp.bfloat16)
    end_terms = jnp.dot(select, layer_out, preferred_element_type=jnp.float32)
    end_rows = lax.psum_scatter(
        end_terms.astype(jnp.bfloat16), "tensor", scatter_dimension=1, tiled=True
    )
    table = lax.all_gather(end_rows, "dp", axis=0, tiled=True)
    pick = (request_prompt[:, None] == jnp.arange(table.shape[0], dtype=jnp.int32)[None, :]).astype(
        jnp.bfloat16
    )
    request_state = jnp.dot(pick, table, preferred_element_type=jnp.float32).astype(jnp.bfloat16)
    return (layer_out, paged_key_value_cache, request_state)


def fused_kernel(
    lengths_ref,
    page_ref,
    request_ref,
    stream_ref,
    attn_gain_ref,
    query_gain_ref,
    key_gain_ref,
    mlp_gain_ref,
    frequency_ref,
    wq_hbm,
    wkv_hbm,
    wo_hbm,
    wg_hbm,
    wu_hbm,
    wd_hbm,
    layer_ref,
    cache_ref,
    state_ref,
    wq,
    wkv,
    wo,
    wg,
    wu,
    wd,
    gathered,
    q_rot,
    kv_all,
    slots_all,
    attn,
    hidden,
    part,
    y_in,
    z_out,
    z_in,
    cosine,
    sine,
    starts,
    resid,
    end_out,
    end_in,
    table,
    weight_sem,
    ag_recv,
    ag_zsend,
    ag_ysend,
    rs_yrecv,
    rs_ysend,
    rs_zrecv,
    rs_zsend,
    kv_send,
    kv_recv,
    slots_send,
    slots_recv,
    end_send,
    end_recv,
    table_send,
    table_recv,
):
    f32 = jnp.float32
    bf16 = jnp.bfloat16
    t = lax.axis_index("tensor")
    g = lax.axis_index("dp")
    z = t // 2
    y = t % 2
    rows = stream_ref.shape[0]
    width = stream_ref.shape[1]
    tokens = rows * 8

    pairs = ((wq_hbm, wq), (wkv_hbm, wkv), (wo_hbm, wo), (wg_hbm, wg), (wu_hbm, wu), (wd_hbm, wd))
    loads = [
        pltpu.make_async_copy(source, target, weight_sem.at[k])
        for k, (source, target) in enumerate(pairs)
    ]
    for load in loads:
        load.start()

    barrier = pltpu.get_barrier_semaphore()
    for k in range(1, 8):
        pl.semaphore_signal(barrier, inc=1, device_id=(g, (t + k) % 8), device_id_type=MESH)
    for k in range(1, 4):
        pl.semaphore_signal(barrier, inc=1, device_id=((g + k) % 4, t), device_id_type=MESH)

    def normed(value, gain_ref):
        scale = lax.rsqrt(jnp.mean(value * value, axis=-1, keepdims=True) + epsilon)
        gain = gain_ref[...].astype(f32)
        return value * scale * (gain.reshape(1, -1) if gain.ndim == 1 else gain)

    gathered[0, t] = normed(stream_ref[...].astype(f32), attn_gain_ref).astype(bf16)
    pl.semaphore_wait(barrier, 10)

    def y_copy(source, target, send, recv):
        return pltpu.make_async_remote_copy(
            src_ref=source, dst_ref=target, send_sem=send, recv_sem=recv,
            device_id=(g, z * 2 + 1 - y), device_id_type=MESH)

    def z_copy(source, target, send, recv, step):
        return pltpu.make_async_remote_copy(
            src_ref=source, dst_ref=target, send_sem=send, recv_sem=recv,
            device_id=(g, (z + step) * 2 + y), device_id_type=MESH)

    def gather(phase, before, process, after):
        def up(s):
            slot = (z - s) * 2 + y
            return z_copy(gathered.at[phase, slot], gathered.at[phase, slot],
                          ag_zsend.at[phase, 0, s], ag_recv.at[phase, slot], 1)

        def down(s):
            slot = (z + s) * 2 + y
            return z_copy(gathered.at[phase, slot], gathered.at[phase, slot],
                          ag_zsend.at[phase, 1, s], ag_recv.at[phase, slot], -1)

        def across(level):
            slot = level * 2 + y
            return y_copy(gathered.at[phase, slot], gathered.at[phase, slot],
                          ag_ysend.at[phase, level], ag_recv.at[phase, slot])

        def arrived(slot):
            y_copy(gathered.at[phase, slot], gathered.at[phase, slot],
                   ag_ysend.at[phase, 0], ag_recv.at[phase, slot]).wait_recv()

        def group(level):
            arrived(level * 2 + 1 - y)
            process(level)

        def groups(s):
            if s == 0:
                group(z)
            else:
                pl.when(z - s >= 0)(lambda: group(z - s))
                pl.when(z + s <= 3)(lambda: group(z + s))

        for s in range(4):
            if s:
                @pl.when(z - s >= 0)
                def _():
                    arrived((z - s) * 2 + y)

                    @pl.when(z < 3)
                    def _():
                        up(s).start()

                    across(z - s).start()

                @pl.when(z + s <= 3)
                def _():
                    arrived((z + s) * 2 + y)

                    @pl.when(z > 0)
                    def _():
                        down(s).start()

                    across(z + s).start()

                groups(s - 1)
                if s == 3:
                    after()
            else:
                pl.when(z < 3)(lambda: up(0).start())
                pl.when(z > 0)(lambda: down(0).start())
                across(z).start()
                before()
        groups(3)

        for s in range(4):
            pl.when((z - s >= 0) & (z < 3))(lambda: up(s).wait_send())
            pl.when((z + s <= 3) & (z > 0))(lambda: down(s).wait_send())
            across(s).wait_send()

    packed = 27 + 72 * z - 15 * (z * (z - 1) // 2) + 5 * (z * (z - 1) * (z - 2))
    order = [packed % 4, packed // 4 % 4, packed // 16 % 4, packed // 64]

    piece = 512
    pieces = width // piece

    def columns(p):
        return pl.ds(pl.multiple_of(p * piece, piece), piece)

    def send_part(phase, level, p):
        return y_copy(part.at[phase, level, 1 - y, p],
                      y_in.at[phase, level, p],
                      rs_ysend.at[phase, level, p], rs_yrecv.at[phase, level, p])

    def flow(phase, level, direction, step, p):
        return z_copy(z_out.at[phase, level, p],
                      z_in.at[phase, direction, level, p],
                      rs_zsend.at[phase, level, p], rs_zrecv.at[phase, direction, level, p], step)

    def forward(phase, level, p):
        send_part(phase, level, p).wait_recv()
        z_out[phase, level, p] = (
            part[phase, level, y, p].astype(f32) + y_in[phase, level, p].astype(f32)
        ).astype(bf16)

        def onward(direction, step, inner):
            @pl.when(inner)
            def _():
                flow(phase, level, direction, step, p).wait_recv()
                z_out[phase, level, p] = (
                    part[phase, level, y, p].astype(f32)
                    + y_in[phase, level, p].astype(f32)
                    + z_in[phase, direction, level, p].astype(f32)
                ).astype(bf16)

            flow(phase, level, direction, step, p).start()

        pl.when(level > z)(lambda: onward(0, 1, z > 0))
        pl.when(level < z)(lambda: onward(1, -1, z < 3))

    def collect(phase):
        @pl.loop(0, pieces)
        def _(p):
            cols = columns(p)
            send_part(phase, z, p).wait_recv()
            resid[1, :, cols] = (
                part[phase, z, y, p].astype(f32) + y_in[phase, z, p].astype(f32))

            @pl.when(z > 0)
            def _():
                flow(phase, z, 0, 1, p).wait_recv()
                resid[1, :, cols] = resid[1, :, cols] + z_in[phase, 0, z, p].astype(f32)

            @pl.when(z < 3)
            def _():
                flow(phase, z, 1, -1, p).wait_recv()
                resid[1, :, cols] = resid[1, :, cols] + z_in[phase, 1, z, p].astype(f32)

    def sent(phase):
        @pl.loop(0, pieces)
        def _(p):
            for level in range(4):
                send_part(phase, level, p).wait_send()
                pl.when(z != level)(lambda: flow(phase, level, 0, 1, p).wait_send())

    def angles():
        ids = lax.broadcasted_iota(jnp.int32, (tokens, HEAD_SIZE), 0)
        begin = jnp.int32(0)
        offset = jnp.zeros((tokens, HEAD_SIZE), jnp.int32)
        for k in range(lengths_ref.shape[1]):
            end = begin + lengths_ref[0, k]
            offset = jnp.where((ids >= begin) & (ids < end), begin, offset)
            begin = end
        starts[...] = offset
        angle = (ids - offset).astype(f32) * frequency_ref[...]
        lane = lax.broadcasted_iota(jnp.int32, (tokens, HEAD_SIZE), 1)
        cosine[...] = jnp.cos(angle)
        signed = jnp.sin(angle)
        sine[...] = jnp.where(lane < HEAD_SIZE // 2, -signed, signed)
        token = lax.broadcasted_iota(jnp.int32, slots_all.shape[1:], 1)
        slots = jnp.zeros(slots_all.shape[1:], jnp.int32)
        for k in range(page_ref.shape[0]):
            slots = jnp.where(token // PAGE_TOKENS == k, page_ref[k], slots)
        slots_all[0] = slots * PAGE_TOKENS + token % PAGE_TOKENS
        loads[0].wait()
        loads[1].wait()

    heads = wq.shape[1] // HEAD_SIZE

    def project(level):
        inputs = gathered[0, pl.ds(level * 2, 2)].reshape(2 * rows, width)
        span = pl.ds(pl.multiple_of(level * 2 * rows, 32), 2 * rows)
        cos_rows = cosine[span, :]
        sin_rows = sine[span, :]

        def rotated(value):
            return value * cos_rows + pltpu.roll(value, HEAD_SIZE // 2, 1) * sin_rows

        for pair in range(heads // 2):
            block = jnp.dot(inputs, wq[:, pair * 256:(pair + 1) * 256], preferred_element_type=f32)
            for k in range(2):
                head = block[:, k * HEAD_SIZE:(k + 1) * HEAD_SIZE]
                q_rot[pair * 2 + k, span, :] = rotated(normed(head, query_gain_ref)).astype(bf16)
        keyval = jnp.dot(inputs, wkv[...], preferred_element_type=f32).astype(bf16)
        key_head = keyval[:, :HEAD_SIZE].astype(f32)
        kv_all[0, span, :HEAD_SIZE] = rotated(normed(key_head, key_gain_ref)).astype(bf16)
        kv_all[0, span, HEAD_SIZE:] = keyval[:, HEAD_SIZE:]

    gather(0, angles, project, lambda: None)

    def kv_copies(k):
        peer = (lax.rem(g + k, 4), t)
        return (
            pltpu.make_async_remote_copy(
                src_ref=kv_all.at[0], dst_ref=kv_all.at[k], send_sem=kv_send.at[k],
                recv_sem=kv_recv.at[k], device_id=peer, device_id_type=MESH),
            pltpu.make_async_remote_copy(
                src_ref=slots_all.at[0], dst_ref=slots_all.at[k], send_sem=slots_send.at[k],
                recv_sem=slots_recv.at[k], device_id=peer, device_id_type=MESH),
        )

    for k in range(1, 4):
        for copy in kv_copies(k):
            copy.start()

    outer = (z == 0) | (z == 3)

    tile = 256
    group_rows = 2 * rows
    loads[2].wait()
    for i in range(4):
        level = order[i]
        first_row = pl.multiple_of(level * group_rows, 32)
        span = pl.ds(first_row, group_rows)
        row_id = first_row + lax.broadcasted_iota(jnp.int32, (group_rows, tokens), 0)
        key_id = lax.broadcasted_iota(jnp.int32, (group_rows, tokens), 1)
        begin = jnp.concatenate([starts[span, :]] * (tokens // HEAD_SIZE), axis=1)
        allowed = (key_id >= begin) & (key_id <= row_id)
        for head in range(heads):
            scores = lax.dot_general(
                q_rot[head, span, :], kv_all[0, :, :HEAD_SIZE], (((1,), (1,)), ((), ())),
                preferred_element_type=f32) * (1.0 / math.sqrt(HEAD_SIZE))
            scores = jnp.where(allowed, scores, -jnp.inf)
            peak = jnp.max(scores, axis=1, keepdims=True)
            weight = jnp.exp(scores - peak)
            total_weight = jnp.sum(weight, axis=1, keepdims=True)
            mixed = jnp.dot(
                weight.astype(bf16), kv_all[0, :, HEAD_SIZE:], preferred_element_type=f32)
            attn[:, head * HEAD_SIZE:(head + 1) * HEAD_SIZE] = (mixed / total_weight).astype(bf16)
        inputs = attn[...]

        @pl.loop(0, pieces)
        def _(p):
            cols = columns(p)
            out = jnp.dot(inputs, wo[:, cols], preferred_element_type=f32)
            part[0, level, :, p] = out.astype(bf16).reshape(2, rows, piece)
            send_part(0, level, p).start()

        def pass_on(k):
            @pl.loop(0, pieces)
            def _(p):
                forward(0, order[k], p)

        if i >= 1:
            pl.when(outer)(lambda: pass_on(i - 1))
        if i >= 2:
            pl.when(jnp.logical_not(outer))(lambda: pass_on(i - 2))
        if i == 3:
            pl.when(jnp.logical_not(outer))(lambda: pass_on(2))

    collect(0)
    residual = (stream_ref[...].astype(f32) + resid[1]).astype(bf16)
    resid[0] = residual.astype(f32)
    gathered[1, t] = normed(resid[0], mlp_gain_ref).astype(bf16)

    def fill_cache():
        row = g * tokens + lax.broadcasted_iota(jnp.int32, (tokens, tokens), 0)
        total = None
        for k in range(4):
            if k:
                for copy in kv_copies(k):
                    copy.wait()
            pick = (slots_all[k, 0:1, :] == row).astype(f32).astype(bf16)
            term = jnp.dot(pick, kv_all[k], preferred_element_type=f32)
            total = term if total is None else total + term
        cache_ref[...] = total.astype(bf16)
        loads[3].wait()
        loads[4].wait()
        loads[5].wait()

    hidden_width = wg.shape[0]

    across_cols = (((1,), (1,)), ((), ()))

    def feed_forward(level):
        inputs = gathered[1, pl.ds(level * 2, 2)].reshape(2 * rows, width)
        for start in range(0, hidden_width, tile):
            stop = min(start + tile, hidden_width)
            gate = lax.dot_general(inputs, wg[start:stop, :], across_cols, preferred_element_type=f32)
            upward = lax.dot_general(inputs, wu[start:stop, :], across_cols, preferred_element_type=f32)
            hidden[:, start:stop] = (gate / (1.0 + jnp.exp(-gate)) * upward).astype(bf16)
        inner = hidden[...]

        @pl.loop(0, pieces)
        def _(p):
            cols = columns(p)
            out = jnp.dot(inner, wd[:, cols], preferred_element_type=f32)
            part[1, level, :, p] = out.astype(bf16).reshape(2, rows, piece)
            send_part(1, level, p).start()

    def early():
        @pl.when(outer)
        def _():
            @pl.loop(0, pieces)
            def _(p):
                forward(1, order[2], p)

    gather(1, fill_cache, feed_forward, early)

    @pl.when(outer)
    def _():
        for i in (1, 0):

            @pl.loop(0, pieces)
            def _(p):
                forward(1, order[i], p)

    @pl.when(jnp.logical_not(outer))
    def _():
        @pl.loop(0, pieces)
        def _(p):
            forward(1, order[2], p)

        @pl.loop(0, pieces)
        def _(p):
            forward(1, order[0], p)
            forward(1, order[1], p)

    collect(1)
    layer_out = (resid[0] + resid[1]).astype(bf16)
    layer_ref[...] = layer_out

    slots = end_out.shape[1]
    span_cols = end_out.shape[2]
    row_id = t * rows + lax.broadcasted_iota(jnp.int32, (slots, rows), 1)
    slot_id = lax.broadcasted_iota(jnp.int32, (slots, rows), 0)
    end = jnp.int32(0)
    hit = jnp.zeros((slots, rows), f32)
    for k in range(lengths_ref.shape[1]):
        end = end + lengths_ref[0, k]
        hit = jnp.where((slot_id == k) & (row_id == end - 1), 1.0, hit)
    terms = jnp.dot(hit.astype(bf16), layer_out, preferred_element_type=f32).astype(bf16)
    for k in range(8):
        first = k * 5 // 2 * 128
        end_out[k] = terms[:, first:first + span_cols]

    def end_copy(k):
        peer = lax.rem(t + k, 8)
        return pltpu.make_async_remote_copy(
            src_ref=end_out.at[peer], dst_ref=end_in.at[k], send_sem=end_send.at[k],
            recv_sem=end_recv.at[k], device_id=(g, peer), device_id_type=MESH)

    for k in range(1, 8):
        end_copy(k).start()
    total = end_out[t].astype(f32)
    for k in range(1, 8):
        end_copy(k).wait()
        total = total + end_in[k].astype(f32)
    table[0] = total.astype(bf16)

    def table_copy(k):
        return pltpu.make_async_remote_copy(
            src_ref=table.at[0], dst_ref=table.at[k], send_sem=table_send.at[k],
            recv_sem=table_recv.at[k], device_id=(lax.rem(g + k, 4), t), device_id_type=MESH)

    for k in range(1, 4):
        table_copy(k).start()
    prompts = lengths_ref.shape[1]
    requests = request_ref.shape[0]
    line = lax.broadcasted_iota(jnp.int32, (requests, slots), 0)
    column = lax.broadcasted_iota(jnp.int32, (requests, slots), 1)
    asked = jnp.zeros((requests, slots), jnp.int32)
    for k in range(requests):
        asked = jnp.where(line == k, request_ref[k], asked)
    state = None
    for k in range(4):
        if k:
            table_copy(k).wait()
        batch = lax.rem(g + 4 - k, 4)
        pick = ((asked == batch * prompts + column) & (column < prompts)).astype(f32).astype(bf16)
        term = jnp.dot(pick, table[k], preferred_element_type=f32)
        state = term if state is None else state + term
    sent(0)
    sent(1)
    keep = state_ref.shape[1]
    shifted = state[:, span_cols - keep:]
    state_ref[...] = jnp.where(t % 2 == 1, shifted, state[:, :keep]).astype(bf16)


def fused_device(
    stream,
    lengths,
    page_table,
    request_prompt,
    attn_gain,
    query_gain,
    key_gain,
    mlp_gain,
    w_query,
    key_value_weight,
    w_out,
    w_gate,
    w_up,
    w_down,
):
    rows, width = stream.shape
    tokens = rows * 8
    query_cols = w_query.shape[1]
    keyval_cols = key_value_weight.shape[1]
    hidden_width = w_gate.shape[1]
    heads = query_cols // HEAD_SIZE
    requests = request_prompt.shape[0]
    state_cols = width // 8
    pieces = width // 512
    exponents = -2.0 * (np.arange(HEAD_SIZE) % (HEAD_SIZE // 2)) / HEAD_SIZE
    frequency = np.power(rope_base, exponents).astype(np.float32)[None, :]
    bf16 = jnp.bfloat16
    f32 = jnp.float32
    vmem = pl.BlockSpec(memory_space=pltpu.VMEM)
    smem = pl.BlockSpec(memory_space=pltpu.SMEM)
    hbm = pl.BlockSpec(memory_space=pl.ANY)
    dma = pltpu.SemaphoreType.DMA
    layer_out, cache, state = pl.pallas_call(
        fused_kernel,
        out_shape=(
            jax.ShapeDtypeStruct((rows, width), bf16),
            jax.ShapeDtypeStruct((tokens, keyval_cols), bf16),
            jax.ShapeDtypeStruct((requests, state_cols), bf16),
        ),
        in_specs=[smem] * 3 + [vmem] * 6 + [hbm] * 6,
        out_specs=(vmem, vmem, vmem),
        scratch_shapes=[
            pltpu.VMEM((width, query_cols), bf16),
            pltpu.VMEM((width, keyval_cols), bf16),
            pltpu.VMEM((query_cols, width), bf16),
            pltpu.VMEM((hidden_width, width), bf16),
            pltpu.VMEM((hidden_width, width), bf16),
            pltpu.VMEM((hidden_width, width), bf16),
            pltpu.VMEM((2, 8, rows, width), bf16),
            pltpu.VMEM((heads, tokens, HEAD_SIZE), bf16),
            pltpu.VMEM((4, tokens, keyval_cols), bf16),
            pltpu.VMEM((4, 8, tokens), jnp.int32),
            pltpu.VMEM((2 * rows, query_cols), bf16),
            pltpu.VMEM((2 * rows, hidden_width), bf16),
            pltpu.VMEM((2, 4, 2, pieces, rows, 512), bf16),
            pltpu.VMEM((2, 4, pieces, rows, 512), bf16),
            pltpu.VMEM((2, 4, pieces, rows, 512), bf16),
            pltpu.VMEM((2, 2, 4, pieces, rows, 512), bf16),
            pltpu.VMEM((tokens, HEAD_SIZE), f32),
            pltpu.VMEM((tokens, HEAD_SIZE), f32),
            pltpu.VMEM((tokens, HEAD_SIZE), jnp.int32),
            pltpu.VMEM((2, rows, width), f32),
            pltpu.VMEM((8, 16, 384), bf16),
            pltpu.VMEM((8, 16, 384), bf16),
            pltpu.VMEM((4, 16, 384), bf16),
            dma((6,)),
            dma((2, 8)),
            dma((2, 2, 4)),
            dma((2, 4)),
            dma((2, 4, pieces)),
            dma((2, 4, pieces)),
            dma((2, 2, 4, pieces)),
            dma((2, 4, pieces)),
            dma((4,)),
            dma((4,)),
            dma((4,)),
            dma((4,)),
            dma((8,)),
            dma((8,)),
            dma((4,)),
            dma((4,)),
        ],
        compiler_params=pltpu.CompilerParams(
            collective_id=0, has_side_effects=True, vmem_limit_bytes=60 * 1024 * 1024
        ),
        name="fused_layer",
    )(
        lengths, page_table, request_prompt, stream, attn_gain, query_gain[None, :], key_gain[None, :],
        mlp_gain, frequency, w_query, key_value_weight, w_out, w_gate.T, w_up.T, w_down,
    )
    return layer_out, cache.reshape(tokens // PAGE_TOKENS, PAGE_TOKENS, keyval_cols), state


def solution(mesh):
    placed = (
        P(("dp", "tensor"), None),
        P("dp", None),
        P("dp"),
        P("dp"),
        P(),
        P(),
        P(),
        P(),
        P(None, "tensor"),
        P(None, "tensor"),
        P("tensor", None),
        P(None, "tensor"),
        P(None, "tensor"),
        P("tensor", None),
    )
    fused = mesh.shape["tensor"] == KEY_VALUE_HEADS and mesh.shape["dp"] == 4
    return jax.shard_map(
        fused_device if fused else per_device,
        mesh=mesh,
        in_specs=placed,
        out_specs=(P(("dp", "tensor"), None), P("dp", None, "tensor"), P("dp", "tensor")),
        check_vma=False,
    )
```
